512 devices in a mesh: dp: 32 (over y_hi, z, core), expert: 4 (over y_lo), tensor: 4 (over x).
Axes of the slice: x: 4, y: 8 (y_hi: 2, y_lo: 4; y = y_hi * 4 + y_lo), z: 8, core: 2. Of those that a mesh axis runs over, the one named last changes fastest.
Arguments:
- tokens: bfloat16 [8192, 2048], P('dp', ('expert', 'tensor')), may hold values from -6 to 6
- grad_hidden: bfloat16 [8192, 5632], P('dp', ('expert', 'tensor')), may hold values from -6 to 6
- merge_probs: float32 [32, 16], replicated, as said below
- w_gate: bfloat16 [16, 2048, 5632], P(None, 'dp', ('expert', 'tensor')), may hold values from -0.125 to 0.125
- w_up: bfloat16 [16, 2048, 5632], P(None, 'dp', ('expert', 'tensor')), may hold values from -0.125 to 0.125
Outputs:
- grad_tokens: bfloat16 [8192, 2048], P('dp', ('expert', 'tensor'))
- grad_w_gate: bfloat16 [16, 2048, 5632], P(None, 'dp', ('expert', 'tensor'))
- grad_w_up: bfloat16 [16, 2048, 5632], P(None, 'dp', ('expert', 'tensor'))
- grad_probs: float32 [32, 16], replicated
The draws below stay inside these ranges and needn't reach their ends.
Inputs may be any that keep to these rules, and one draw needn't show every extreme that they name: `merge_probs`: every entry is positive and each row sums to 1.
All inputs are finite; a program needn't handle non-finite values.
Results may differ from the reference program's by a relative error of at most 0.0065.
Values may be sent and summed in bfloat16 or wider, within the bound.
A program may use at most 64 MiB of HBM per device.

```python
import jax
import jax.numpy as jnp
from jax import lax

D = 2048
FF = 5632
E = 16
SEG = 256
SEGMENTS = 32
TOKENS = 8192


def draw_merge_probs(key, part):
    key = jax.random.fold_in(key, 7)
    logits = 1.5 * jax.random.normal(key, (SEGMENTS, E), jnp.float32)
    weights = jnp.exp(logits)
    return weights / jnp.sum(weights, axis=1, keepdims=True)


def shard_levels(key, dims, split, low, largest):
    level, own = 1.0, jax.random.fold_in(key, 6)
    for axis_at, shards_of in split:
        steps = jnp.exp(jax.random.uniform(jax.random.fold_in(own, axis_at), (shards_of,), jnp.float32, low / len(split), largest / len(split)))
        level = level * jnp.repeat(steps, dims[axis_at] // shards_of).reshape([-1 if axis == axis_at else 1 for axis in range(len(dims))])
    return level


def normal_values(own_key, shape, width, most, cuts=(), held_as=jnp.bfloat16):
    drawn = width * jax.random.normal(own_key, shape, jnp.float32)
    if cuts:
        drawn = drawn * shard_levels(own_key, shape, cuts, -0.22, 0.18)
    return jnp.clip(drawn, -most, most).astype(held_as)


def setup_inputs(seed: int = 0) -> dict:
    arg_keys = jax.random.split(jax.random.key(seed), 6)
    tokens = normal_values(arg_keys[0], (TOKENS, D), 1.0, 6.0, ((0, 32), (1, 16)))
    grad_hidden = normal_values(arg_keys[1], (TOKENS, FF), 1.0, 6.0, ((0, 32), (1, 16)))
    merge_probs = draw_merge_probs(jax.random.fold_in(arg_keys[5], 71), 0)
    w_gate = normal_values(arg_keys[3], (E, D, FF), D ** -0.5, 0.125, ((1, 32), (2, 16)))
    w_up = normal_values(arg_keys[4], (E, D, FF), D ** -0.5, 0.125, ((1, 32), (2, 16)))
    return dict(tokens=tokens, grad_hidden=grad_hidden, merge_probs=merge_probs, w_gate=w_gate, w_up=w_up)


def reference(tokens, grad_hidden, merge_probs, w_gate, w_up):
    highest = lax.Precision.HIGHEST
    seg_tokens_all = tokens.reshape(SEGMENTS, SEG, D)
    seg_cot_all = grad_hidden.reshape(SEGMENTS, SEG, FF)

    def segment_pass(running, inputs):
        sum_gate, sum_up = running
        seg_tokens, seg_cot, seg_weights = inputs
        merged_gate = jnp.tensordot(seg_weights, w_gate.astype(jnp.float32), axes=1, precision=highest).astype(jnp.bfloat16)
        merged_up = jnp.tensordot(seg_weights, w_up.astype(jnp.float32), axes=1, precision=highest).astype(jnp.bfloat16)
        gate_pre = jnp.dot(seg_tokens, merged_gate, preferred_element_type=jnp.float32)
        up_pre = jnp.dot(seg_tokens, merged_up, preferred_element_type=jnp.float32)
        sig_gate = jax.nn.sigmoid(gate_pre)
        upstream = seg_cot.astype(jnp.float32)
        grad_gate = (upstream * up_pre * sig_gate * (1.0 + gate_pre * (1.0 - sig_gate))).astype(jnp.bfloat16)
        grad_up = (upstream * gate_pre * sig_gate).astype(jnp.bfloat16)
        grad_rows = jnp.dot(grad_gate, merged_gate.T, preferred_element_type=jnp.float32)
        grad_rows = (grad_rows + jnp.dot(grad_up, merged_up.T, preferred_element_type=jnp.float32)).astype(jnp.bfloat16)
        merged_grad_gate = jnp.dot(seg_tokens.T, grad_gate, preferred_element_type=jnp.float32).astype(jnp.bfloat16)
        merged_grad_up = jnp.dot(seg_tokens.T, grad_up, preferred_element_type=jnp.float32).astype(jnp.bfloat16)
        merged_grad_gate = lax.optimization_barrier(merged_grad_gate).astype(jnp.float32)
        merged_grad_up = lax.optimization_barrier(merged_grad_up).astype(jnp.float32)
        sum_gate = sum_gate + seg_weights[:, None, None] * merged_grad_gate[None]
        sum_up = sum_up + seg_weights[:, None, None] * merged_grad_up[None]
        probs_grad = jnp.tensordot(w_gate.astype(jnp.float32), merged_grad_gate, axes=([1, 2], [0, 1]), precision=highest)
        probs_grad = probs_grad + jnp.tensordot(w_up.astype(jnp.float32), merged_grad_up, axes=([1, 2], [0, 1]), precision=highest)
        return (sum_gate, sum_up), (grad_rows, probs_grad)

    zeros_init = jnp.zeros((E, D, FF), jnp.float32)
    (sum_gate, sum_up), (grad_rows, grad_probs) = lax.scan(segment_pass, (zeros_init, zeros_init), (seg_tokens_all, seg_cot_all, merge_probs))
    grad_tokens = grad_rows.reshape(TOKENS, D)
    return grad_tokens, sum_gate.astype(jnp.bfloat16), sum_up.astype(jnp.bfloat16), grad_probs
```

```python
import functools

import jax
import jax.numpy as jnp
from jax import lax
from jax.experimental import pallas as pl
from jax.experimental.pallas import tpu as pltpu
from jax.sharding import PartitionSpec as P

MESH = pl.DeviceIdType.MESH
F32, BF16 = jnp.float32, jnp.bfloat16
HIGHEST = lax.Precision.HIGHEST
VMEM = pl.BlockSpec(memory_space=pltpu.VMEM)
DMA = pltpu.SemaphoreType.DMA
NZ, NY, NX, G = 8, 8, 4, 16
TN = (((0,), (0,)), ((), ()))
NT = (((1,), (1,)), ((), ()))


class Place:
    def __init__(self):
        d = lax.axis_index("dp")
        self.h, self.z, self.c = d // 16, (d // 2) % 8, d % 2
        self.e, self.x = lax.axis_index("expert"), lax.axis_index("tensor")
        self.y = 4 * self.h + self.e

    def at(self, h=None, z=None, c=None, e=None, x=None):
        h = self.h if h is None else h
        z = self.z if z is None else z
        c = self.c if c is None else c
        return {
            "dp": h * 16 + z * 2 + c,
            "expert": self.e if e is None else e,
            "tensor": self.x if x is None else x,
        }

    def sibling(self):
        return self.at(c=1 - self.c)

    def far(self):
        return self.at(h=1 - self.h)

    def at_y(self, step):
        y = (self.y + step) % NY
        return self.at(h=y // 4, e=y % 4)

    def at_z(self, step):
        return self.at(z=(self.z + step + NZ) % NZ)

    def at_x(self, step):
        return self.at(x=(self.x + step) % NX)

    def swapped(self):
        z = 4 * (self.e % 2) + self.x
        e = 2 * (self.e // 2) + self.z // 4
        return self.at(z=z, e=e, x=self.z % 4), z == self.z


def greet(peers, swap=None):
    barrier = pltpu.get_barrier_semaphore()
    for peer in peers:
        pl.semaphore_signal(barrier, inc=1, device_id=peer, device_id_type=MESH)
    count = len(peers)
    if swap is not None:
        peer, own = swap
        count = count + jnp.where(own, 0, 1)

        @pl.when(jnp.logical_not(own))
        def _():
            pl.semaphore_signal(barrier, inc=1, device_id=peer, device_id_type=MESH)

    pl.semaphore_wait(barrier, count)


def remote(src, dst, send, recv, peer):
    return pltpu.make_async_remote_copy(
        src_ref=src, dst_ref=dst, send_sem=send, recv_sem=recv, device_id=peer, device_id_type=MESH
    )


def swap_start(swap, src, dst, sems):
    peer, own = swap

    @pl.when(own)
    def _():
        pltpu.make_async_copy(src, dst, sems.at[0]).start()

    @pl.when(jnp.logical_not(own))
    def _():
        remote(src, dst, sems.at[1], sems.at[2], peer).start()


def swap_wait(swap, src, dst, sems):
    peer, own = swap

    @pl.when(own)
    def _():
        pltpu.make_async_copy(src, dst, sems.at[0]).wait()

    @pl.when(jnp.logical_not(own))
    def _():
        remote(src, dst, sems.at[1], sems.at[2], peer).wait()


def dot(a, b, dims=(((1,), (0,)), ((), ())), precision=None):
    return lax.dot_general(a, b, dims, preferred_element_type=F32, precision=precision)


def one_hot(shape, row_div, col_div, dtype):
    rows = lax.broadcasted_iota(jnp.int32, shape, 0) // row_div
    cols = lax.broadcasted_iota(jnp.int32, shape, 1) // col_div
    return jnp.where(rows == cols, 1.0, 0.0).astype(dtype)


def diagonal():
    rows = lax.broadcasted_iota(jnp.int32, (256, 256), 0) % G
    cols = lax.broadcasted_iota(jnp.int32, (256, 256), 1) % G
    return rows == cols


def spread(table, mask, transpose):
    wide = one_hot((256, 16), G, 1, BF16)
    high = table.astype(BF16)
    low = (table - high.astype(F32)).astype(BF16)
    out = []
    for part in (high, low):
        if transpose:
            half = dot(wide, part, NT).astype(BF16)
        else:
            half = dot(wide, part).astype(BF16)
        full = dot(half, wide, NT)
        out.append(jnp.where(mask, full, 0.0).astype(BF16))
    return out


def merge_kernel(
    w_ref, xt_ref, p_ref, m_ref, x_ref, far_ref, table, staged,
    swap_sems, y_send, y_recv, x_send, x_recv, far_send, far_recv, sib_send, sib_recv,
):
    me = Place()
    swap = me.swapped()
    greet(
        [me.sibling()] + [me.at_y(i) for i in range(1, NY)] + [me.at_x(i) for i in range(1, NX)],
        swap,
    )
    far = []
    for g in range(4):
        far.append(
            remote(
                w_ref.at[1 - me.h, :, pl.ds(G * g, G), :], far_ref.at[:, pl.ds(G * g, G), :],
                far_send.at[g], far_recv.at[g], me.far(),
            )
        )
    there = x_ref.at[2 * me.h + me.z // 4, me.z % 4, pl.ds(pl.multiple_of(128 * (me.e // 2), 128), 128), :]
    mine = x_ref.at[2 * me.h + me.e % 2, me.x, pl.ds(pl.multiple_of(128 * (me.e // 2), 128), 128), :]
    swap_start(swap, xt_ref, there, swap_sems)
    for copy in far:
        copy.start()

    mask = diagonal()
    for seg_core in range(2):
        high, low = spread(p_ref[seg_core], mask, False)
        table[seg_core, 0] = high
        table[seg_core, 1] = low

    sib = []

    def merged(load, j, row, g):
        w = load(g).reshape(256, 352)
        other = dot(table[1 - me.c, 0], w) + dot(table[1 - me.c, 1], w)
        staged[j, :, pl.ds(G * g, G), :] = other.reshape(16, G, 352).astype(BF16)
        at = pl.ds(pl.multiple_of(row + G * g, G), G)
        i = 4 * j + g
        copy = remote(
            staged.at[j, :, pl.ds(G * g, G), :], m_ref.at[:, at, :], sib_send.at[i], sib_recv.at[i],
            me.sibling(),
        )
        copy.start()
        sib.append(copy)
        own = dot(table[me.c, 0], w) + dot(table[me.c, 1], w)
        m_ref[:, at, :] = own.reshape(16, G, 352).astype(BF16)

    for g in range(4):
        merged(lambda g: w_ref[me.h, :, G * g : G * g + G, :], 0, me.h * 128 + me.c * 64, g)

    swap_wait(swap, xt_ref, mine, swap_sems)
    along_y = []
    for i in range(1, NY):
        copy = remote(mine, mine, y_send.at[i - 1], y_recv.at[i - 1], me.at_y(i))
        copy.start()
        along_y.append(copy)
    for copy in along_y:
        copy.wait_recv()
    along_x = []
    for i in range(1, NX):
        own = x_ref.at[:, me.x]
        copy = remote(own, own, x_send.at[i - 1], x_recv.at[i - 1], me.at_x(i))
        copy.start()
        along_x.append(copy)
    for g in range(4):
        far[g].wait_recv()
        merged(lambda g: far_ref[:, G * g : G * g + G, :], 1, (1 - me.h) * 128 + me.c * 64, g)
    for copy in along_x:
        copy.wait()
    for copy in along_y + far:
        copy.wait_send()
    for copy in sib:
        copy.wait()


STREAMS = ((1, 0, 4), (-1, 1, 4), (-1, 0, 3), (1, 1, 3))


def grads_kernel(
    m_ref, x_ref, gh_ref, full_ref, sib_ref, rows_ref, gh_in, sums_out, sums_in, grads,
    gh_sems, rs_send, rs_recv, ag_send, ag_recv, sib_send, sib_recv,
):
    me = Place()
    greet([me.sibling(), me.far(), me.at_z(1), me.at_z(-1)])
    gh_copy = remote(
        gh_ref.at[pl.ds(pl.multiple_of((1 - me.h) * 176, 16), 176), :], gh_in,
        gh_sems.at[0], gh_sems.at[1], me.far(),
    )
    gh_copy.start()

    def level(step):
        return (me.z + step + NZ) % NZ

    def part(half, z):
        return dot(m_ref[8 * half + z], x_ref[2 * half + z // 4, z % 4], TN)

    index = {}
    for direction, half, steps in STREAMS:
        for t in range(steps):
            index[direction, half, t] = len(index)

    copies = []
    last = {}
    for t in range(4):
        for direction, half, steps in STREAMS:
            if t >= steps:
                continue
            i = index[direction, half, t]
            total = part(half, level(direction * (steps - t)))
            if t > 0:
                last[direction, half].wait_recv()
                total = total + sums_in[index[direction, half, t - 1]].astype(F32)
            sums_out[i] = total.astype(BF16)
            copy = remote(sums_out.at[i], sums_in.at[i], rs_send.at[i], rs_recv.at[i], me.at_z(direction))
            copy.start()
            copies.append(copy)
            last[direction, half] = copy

    own_gh = pl.ds(pl.multiple_of(me.h * 176, 16), 176)
    gathers = {}

    def gather(direction, half, t):
        i = index[direction, half, t]
        block = grads.at[half, level(-direction * t)]
        copy = remote(block, block, ag_send.at[i], ag_recv.at[i], me.at_z(direction))
        copy.start()
        gathers[direction, half, t] = copy

    gh_copy.wait_recv()
    for half in range(2):
        pre = part(half, me.z)
        for direction, stream_half, steps in STREAMS:
            if stream_half == half:
                last[direction, half].wait_recv()
                pre = pre + sums_in[index[direction, half, steps - 1]].astype(F32)
        gate, up = pre[:176], pre[176:]
        g = jnp.where(me.h == half, gh_ref[own_gh, :].astype(F32), gh_in[...].astype(F32))
        sig = 1.0 / (1.0 + jnp.exp(-gate))
        grads[half, me.z, 0:176, :] = (g * up * sig * (1.0 + gate * (1.0 - sig))).astype(BF16)
        grads[half, me.z, 176:352, :] = (g * gate * sig).astype(BF16)
        for direction, stream_half, steps in STREAMS:
            if stream_half == half:
                gather(direction, half, 0)

    sib = []

    def back(half, z):
        k = 8 * half + z
        at = (2 * half + z // 4, z % 4)
        block = grads[half, z]
        full_ref[k] = dot(x_ref[at], block, NT).astype(BF16).reshape(2, 2, 64, 352)
        i = len(sib)
        copy = remote(full_ref.at[k, :, 1 - me.c], sib_ref.at[k], sib_send.at[i], sib_recv.at[i], me.sibling())
        copy.start()
        sib.append(copy)
        rows_ref[at] = dot(m_ref[k], block).astype(BF16)

    back(0, me.z)
    back(1, me.z)
    for t in range(4):
        for direction, half, steps in STREAMS:
            if t >= steps:
                continue
            gathers[direction, half, t].wait_recv()
            if t + 1 < steps:
                gather(direction, half, t + 1)
            back(half, level(-direction * (t + 1)))
    for copy in copies + list(gathers.values()) + [gh_copy]:
        copy.wait_send()
    for copy in sib:
        copy.wait()


def output_kernel(
    full_ref, sib_ref, rows_ref, w_ref, far_ref, p_ref, gw_ref, gt_ref, gp_ref,
    table, staged, rows_in, half_sum, slices_in, done, home, probs, ring,
    x_send, x_recv, y_send, y_recv, swap_sems, far_send, far_recv, p_send, p_recv,
):
    me = Place()
    swap = me.swapped()
    greet(
        [me.sibling()] + [me.at_y(i) for i in range(1, NY)] + [me.at_x(i) for i in range(1, NX)]
        + [me.at_z(i) for i in range(1, NZ)],
        swap,
    )
    along_x = []
    for i in range(1, NX):
        copy = remote(
            rows_ref.at[:, (me.x + i) % NX], rows_in.at[i - 1], x_send.at[i - 1], x_recv.at[i - 1], me.at_x(i)
        )
        copy.start()
        along_x.append(copy)

    mask = diagonal()
    for seg_core in range(2):
        high, low = spread(p_ref[seg_core], mask, True)
        table[seg_core, 0] = high
        table[seg_core, 1] = low

    probs[...] = jnp.zeros_like(probs)
    far = []

    def rows(half, g, weights):
        mine = full_ref[:, half, me.c, G * g : G * g + G, :].reshape(256, 352)
        theirs = sib_ref[:, half, G * g : G * g + G, :].reshape(256, 352)
        total = dot(table[me.c, 0], mine) + dot(table[me.c, 1], mine)
        total = total + (dot(table[1 - me.c, 0], theirs) + dot(table[1 - me.c, 1], theirs))
        probs[me.c] += dot(weights, mine, NT)
        probs[1 - me.c] += dot(weights, theirs, NT)
        return total.reshape(16, G, 352).astype(BF16)

    for g in range(4):
        cut = slice(G * g, G * g + G)
        staged[:, cut, :] = rows(1 - me.h, g, far_ref[:, cut, :].reshape(256, 352))
        copy = remote(
            staged.at[:, pl.ds(G * g, G), :], gw_ref.at[me.h, :, pl.ds(G * g, G), :],
            far_send.at[g], far_recv.at[g], me.far(),
        )
        copy.start()
        far.append(copy)
    for g in range(4):
        cut = slice(G * g, G * g + G)
        gw_ref[me.h, :, cut, :] = rows(me.h, g, w_ref[me.h, :, cut, :].reshape(256, 352))

    narrow = one_hot((256, 16), G, 1, F32)
    across = one_hot((256, 128), G, 1, F32)
    local = []
    for seg_core in range(2):
        kept = jnp.where(mask, probs[seg_core], 0.0)
        local.append(dot(dot(narrow, kept, TN, HIGHEST), across, precision=HIGHEST))
    value = jnp.concatenate(local, axis=0)
    used = 0
    waits = []

    def sum_over(value, used, base, place, count, peer):
        ring[base + place] = value
        copies = []
        for i in range(1, count):
            block = ring.at[base + place]
            copy = remote(block, block, p_send.at[used + i - 1], p_recv.at[used + i - 1], peer(i))
            copy.start()
            copies.append(copy)
        for copy in copies:
            copy.wait()
        total = ring[base]
        for i in range(1, count):
            total = total + ring[base + i]
        return total

    value = sum_over(value, 0, 0, me.c, 2, lambda i: me.sibling())
    value = sum_over(value, 1, 2, me.x, NX, me.at_x)

    for copy in along_x:
        copy.wait_recv()
    for lead in range(4):
        total = rows_ref[lead, me.x].astype(F32)
        for i in range(NX - 1):
            total = total + rows_in[i, lead].astype(F32)
        half_sum[lead] = total.astype(BF16)

    def slice_of(y):
        return half_sum.at[2 * (y // 4) + y % 2, pl.ds(pl.multiple_of(128 * ((y % 4) // 2), 128), 128), :]

    along_y = []
    for i in range(1, NY):
        y = (me.y + i) % NY
        copy = remote(slice_of(y), slices_in.at[i - 1], y_send.at[i - 1], y_recv.at[i - 1], me.at_y(i))
        copy.start()
        along_y.append(copy)
    value = sum_over(value, 4, 6, me.y, NY, me.at_y)
    value = sum_over(value, 11, 14, me.z, NZ, me.at_z)
    gp_ref[...] = value
    total = slice_of(me.y)[...].astype(F32)
    for i in range(NY - 1):
        along_y[i].wait_recv()
        total = total + slices_in[i].astype(F32)
    done[...] = total.astype(BF16)
    swap_start(swap, done, home, swap_sems)
    swap_wait(swap, done, home, swap_sems)
    gt_ref[...] = home[...]
    for copy in along_x + along_y:
        copy.wait_send()
    for copy in far:
        copy.wait()


def call(kernel, number, out_shape, scratch, flops, *operands):
    return pl.pallas_call(
        kernel,
        out_shape=out_shape,
        in_specs=[VMEM] * len(operands),
        out_specs=[VMEM] * len(out_shape),
        scratch_shapes=scratch,
        compiler_params=pltpu.CompilerParams(
            collective_id=number, has_side_effects=True, vmem_limit_bytes=50 * 1024 * 1024
        ),
        cost_estimate=pl.CostEstimate(flops=flops, bytes_accessed=8 << 20, transcendentals=0),
    )(*operands)


def shape(*dims, dtype=BF16):
    return jax.ShapeDtypeStruct(dims, dtype)


def shards(tokens, grad_hidden, merge_probs, w_gate, w_up):
    halves = jnp.stack(
        [
            jnp.concatenate([w_gate[..., :176], w_up[..., :176]], axis=-1),
            jnp.concatenate([w_gate[..., 176:], w_up[..., 176:]], axis=-1),
        ]
    )
    probs = merge_probs.reshape(16, 2, 16).transpose(1, 0, 2)
    m, x, far = call(
        merge_kernel, 1,
        [shape(16, 256, 352), shape(4, 4, 256, 256), shape(16, 64, 352)],
        [
            pltpu.VMEM((2, 2, 256, 256), BF16), pltpu.VMEM((2, 16, 64, 352), BF16),
            DMA((3,)), DMA((7,)), DMA((7,)), DMA((3,)), DMA((3,)), DMA((4,)), DMA((4,)), DMA((8,)), DMA((8,)),
        ],
        2 << 30, halves, tokens.T, probs,
    )
    full, sib, rows = call(
        grads_kernel, 2,
        [shape(16, 2, 2, 64, 352), shape(16, 2, 64, 352), shape(4, 4, 256, 256)],
        [
            pltpu.VMEM((176, 256), BF16), pltpu.VMEM((14, 352, 256), BF16), pltpu.VMEM((14, 352, 256), BF16),
            pltpu.VMEM((2, 8, 352, 256), BF16),
            DMA((2,)), DMA((14,)), DMA((14,)), DMA((14,)), DMA((14,)), DMA((16,)), DMA((16,)),
        ],
        2 << 30, m, x, grad_hidden.T,
    )
    gw, gt, gp = call(
        output_kernel, 3,
        [shape(2, 16, 64, 352), shape(128, 256), shape(32, 128, dtype=F32)],
        [
            pltpu.VMEM((2, 2, 256, 256), BF16), pltpu.VMEM((16, 64, 352), BF16),
            pltpu.VMEM((3, 4, 256, 256), BF16), pltpu.VMEM((4, 256, 256), BF16), pltpu.VMEM((7, 128, 256), BF16),
            pltpu.VMEM((128, 256), BF16), pltpu.VMEM((128, 256), BF16), pltpu.VMEM((2, 256, 256), F32),
            pltpu.VMEM((22, 32, 128), F32),
            DMA((3,)), DMA((3,)), DMA((7,)), DMA((7,)), DMA((3,)), DMA((4,)), DMA((4,)), DMA((18,)), DMA((18,)),
        ],
        2 << 30, full, sib, rows, halves, far, probs,
    )
    grad_gate = jnp.concatenate([gw[0, ..., :176], gw[1, ..., :176]], axis=-1)
    grad_up = jnp.concatenate([gw[0, ..., 176:], gw[1, ..., 176:]], axis=-1)
    grad_probs = gp[:, :16].reshape(2, 16, 16).transpose(2, 0, 1).reshape(32, 16)
    return gt.T, grad_gate, grad_up, grad_probs


def solution(mesh):
    return jax.shard_map(
        shards,
        mesh=mesh,
        in_specs=(
            P("dp", ("expert", "tensor")),
            P("dp", ("expert", "tensor")),
            P(),
            P(None, "dp", ("expert", "tensor")),
            P(None, "dp", ("expert", "tensor")),
        ),
        out_specs=(
            P("dp", ("expert", "tensor")),
            P(None, "dp", ("expert", "tensor")),
            P(None, "dp", ("expert", "tensor")),
            P(),
        ),
        check_vma=False,
    )
```

```python
import functools

import jax
import jax.numpy as jnp
from jax import lax
from jax.experimental import pallas as pl
from jax.experimental.pallas import tpu as pltpu
from jax.sharding import PartitionSpec as P

MESH = pl.DeviceIdType.MESH
F32, BF16 = jnp.float32, jnp.bfloat16
HIGHEST = lax.Precision.HIGHEST
VMEM = pl.BlockSpec(memory_space=pltpu.VMEM)
DMA = pltpu.SemaphoreType.DMA
NZ, NY, NX, G = 8, 8, 4, 16
TN = (((0,), (0,)), ((), ()))
NT = (((1,), (1,)), ((), ()))


class Place:
    def __init__(self):
        d = lax.axis_index("dp")
        self.h, self.z, self.c = d // 16, (d // 2) % 8, d % 2
        self.e, self.x = lax.axis_index("expert"), lax.axis_index("tensor")
        self.y = 4 * self.h + self.e

    def at(self, h=None, z=None, c=None, e=None, x=None):
        h = self.h if h is None else h
        z = self.z if z is None else z
        c = self.c if c is None else c
        return {
            "dp": h * 16 + z * 2 + c,
            "expert": self.e if e is None else e,
            "tensor": self.x if x is None else x,
        }

    def sibling(self):
        return self.at(c=1 - self.c)

    def far(self):
        return self.at(h=1 - self.h)

    def at_y(self, step):
        y = (self.y + step) % NY
        return self.at(h=y // 4, e=y % 4)

    def at_z(self, step):
        return self.at(z=(self.z + step + NZ) % NZ)

    def at_x(self, step):
        return self.at(x=(self.x + step) % NX)

    def swapped(self):
        z = 4 * (self.e % 2) + self.x
        e = 2 * (self.e // 2) + self.z // 4
        return self.at(z=z, e=e, x=self.z % 4), z == self.z


def greet(peers, swap=None):
    barrier = pltpu.get_barrier_semaphore()
    for peer in peers:
        pl.semaphore_signal(barrier, inc=1, device_id=peer, device_id_type=MESH)
    count = len(peers)
    if swap is not None:
        peer, own = swap
        count = count + jnp.where(own, 0, 1)

        @pl.when(jnp.logical_not(own))
        def _():
            pl.semaphore_signal(barrier, inc=1, device_id=peer, device_id_type=MESH)

    pl.semaphore_wait(barrier, count)


def remote(src, dst, send, recv, peer):
    return pltpu.make_async_remote_copy(
        src_ref=src, dst_ref=dst, send_sem=send, recv_sem=recv, device_id=peer, device_id_type=MESH
    )


def swap_start(swap, src, dst, sems):
    peer, own = swap

    @pl.when(own)
    def _():
        pltpu.make_async_copy(src, dst, sems.at[0]).start()

    @pl.when(jnp.logical_not(own))
    def _():
        remote(src, dst, sems.at[1], sems.at[2], peer).start()


def swap_wait(swap, src, dst, sems):
    peer, own = swap

    @pl.when(own)
    def _():
        pltpu.make_async_copy(src, dst, sems.at[0]).wait()

    @pl.when(jnp.logical_not(own))
    def _():
        remote(src, dst, sems.at[1], sems.at[2], peer).wait()


def dot(a, b, dims=(((1,), (0,)), ((), ())), precision=None):
    return lax.dot_general(a, b, dims, preferred_element_type=F32, precision=precision)


def one_hot(shape, row_div, col_div, dtype):
    rows = lax.broadcasted_iota(jnp.int32, shape, 0) // row_div
    cols = lax.broadcasted_iota(jnp.int32, shape, 1) // col_div
    return jnp.where(rows == cols, 1.0, 0.0).astype(dtype)


def diagonal():
    rows = lax.broadcasted_iota(jnp.int32, (256, 256), 0) % G
    cols = lax.broadcasted_iota(jnp.int32, (256, 256), 1) % G
    return rows == cols


def pick(core):
    rows = lax.broadcasted_iota(jnp.int32, (256, 32), 0) // G
    cols = lax.broadcasted_iota(jnp.int32, (256, 32), 1)
    return rows * 2 + core == cols


def spread(table, core, mask, transpose):
    experts = one_hot((256, 16), G, 1, BF16)
    segments = jnp.where(pick(core), 1.0, 0.0).astype(BF16)
    high = table.astype(BF16)
    low = (table - high.astype(F32)).astype(BF16)
    out = []
    for part in (high, low):
        if transpose:
            full = dot(dot(experts, part, NT).astype(BF16), segments, NT)
        else:
            full = dot(dot(segments, part).astype(BF16), experts, NT)
        out.append(jnp.where(mask, full, 0.0).astype(BF16))
    return out


STREAMS = ((1, 0, 4), (-1, 1, 4), (-1, 0, 3), (1, 1, 3))
CHUNKS = (128, 128, 96)
LEAD = 3
INDEX = {}
for _direction, _half, _steps in STREAMS:
    for _t in range(_steps):
        INDEX[_direction, _half, _t] = len(INDEX)


def whole_kernel(
    wg_ref, wu_ref, tok_ref, grad_ref, p_ref,
    gt_ref, gg_ref, gu_ref, gp_ref,
    xt_ref, gh_ref, w0, w1, w2, wf0, wf1, wf2, gw0, gw1, gw2,
    forth, back_table, x_ref, gh_in, probs, ring,
    far0, far1, far2, st0, st1, st2, m0, m1, m2, so0, so1, so2, si0, si1, si2, gr0, gr1, gr2,
    full0, full1, full2, sib0, sib1, sib2, gs0, gs1, gs2,
    rows, rows_in, half_sum, slices_in, done, home,
    swap1, swap2, y_send, y_recv, x_send, x_recv, far_send, far_recv, m_send, m_recv, gh_sems,
    rs_send, rs_recv, ag_send, ag_recv, sib_send, sib_recv, out_send, out_recv,
    rx_send, rx_recv, ry_send, ry_recv, p_send, p_recv,
):
    w, w_far, gw = (w0, w1, w2), (wf0, wf1, wf2), (gw0, gw1, gw2)
    far_in, staged, m = (far0, far1, far2), (st0, st1, st2), (m0, m1, m2)
    sums_out, sums_in, grads = (so0, so1, so2), (si0, si1, si2), (gr0, gr1, gr2)
    full, sib_in, gw_out = (full0, full1, full2), (sib0, sib1, sib2), (gs0, gs1, gs2)
    me = Place()
    swap = me.swapped()
    greet(
        [me.sibling()] + [me.at_y(i) for i in range(1, NY)] + [me.at_x(i) for i in range(1, NX)]
        + [me.at_z(i) for i in range(1, NZ)],
        swap,
    )
    sent = []

    def push(src, dst, send, recv, peer):
        copy = remote(src, dst, send, recv, peer)
        copy.start()
        sent.append(copy)
        return copy

    def slot(y, x):
        row = pl.multiple_of(128 * ((y % 4) // 2), 128)
        return x_ref.at[2 * (y // 4) + y % 2, x, pl.ds(row, 128), :]

    def push_far(j):
        return push(w_far[j], far_in[j], far_send.at[j], far_recv.at[j], me.far())

    there = x_ref.at[
        2 * me.h + me.z // 4, me.z % 4, pl.ds(pl.multiple_of(128 * (me.e // 2), 128), 128), :
    ]
    mine = slot(me.y, me.x)
    xt_ref[...] = tok_ref[...].T
    swap_start(swap, xt_ref, there, swap1)

    def pack(half, into):
        tile = pl.ds(pl.multiple_of(128 * half, 128), 128)
        for lo in range(0, 16, 4):
            at = slice(lo, lo + 4)
            gate, up = wg_ref[at, :, tile], wu_ref[at, :, tile]
            into[0][at] = jnp.concatenate([gate[..., :64], up[..., :64]], axis=-1)
            into[1][at] = jnp.concatenate([gate[..., 64:], up[..., 64:]], axis=-1)
            gate, up = wg_ref[at, :, 256:352], wu_ref[at, :, 256:352]
            gate = jnp.where(half == 0, gate[..., :48], gate[..., 48:])
            up = jnp.where(half == 0, up[..., :48], up[..., 48:])
            into[2][at] = jnp.concatenate([gate, up], axis=-1)

    pack(1 - me.h, w_far)
    far = [push_far(0)]
    pack(me.h, w)
    gh_ref[...] = grad_ref[...].T
    mask = diagonal()
    for seg_core in range(2):
        forth[seg_core, 0], forth[seg_core, 1] = spread(p_ref[...], seg_core, mask, False)
    from_sib = {}

    def merge(j, n):
        half = me.h if n == 0 else 1 - me.h
        at = pl.multiple_of(half * 128 + me.c * 64, 64)
        for other in (True, False):
            core = 1 - me.c if other else me.c
            for g in range(4):
                cut = slice(G * g, G * g + G)
                raw = w[j][:, cut, :] if n == 0 else far_in[j][:, cut, :]
                raw = raw.reshape(256, CHUNKS[j])
                out = dot(forth[core, 0], raw) + dot(forth[core, 1], raw)
                out = out.reshape(16, G, CHUNKS[j]).astype(BF16)
                if other:
                    staged[j][n, :, cut, :] = out
                else:
                    m[j][:, pl.ds(pl.multiple_of(at + G * g, G), G), :] = out
            if other:
                i = 2 * j + n
                from_sib[j, n] = push(
                    staged[j].at[n], m[j].at[:, pl.ds(at, 64), :], m_send.at[i], m_recv.at[i], me.sibling()
                )

    merge(0, 0)
    swap_wait(swap, xt_ref, mine, swap1)
    along_y, along_x = {}, []

    def push_x(n):
        block = slot((me.y - n + NY) % NY, me.x)
        for i in range(1, NX):
            k = (i - 1) * NY + n
            along_x.append(push(block, block, x_send.at[k], x_recv.at[k], me.at_x(i)))

    for i in (1, 7, 2, 6, 3, 5, 4):
        along_y[i] = push(mine, mine, y_send.at[i - 1], y_recv.at[i - 1], me.at_y(i))
    push_x(0)
    merge(1, 0)
    merge(2, 0)
    for i in (1, 7, 2, 6, 3, 5, 4):
        along_y[i].wait_recv()
        push_x(i)
    far += [push_far(1), push_far(2)]
    gh_copies = []
    for n, (base, step, size) in enumerate(((0, 128, 128), (256, 48, 48))):
        rows_there = pl.ds(pl.multiple_of(base + step * (1 - me.h), 16), size)
        gh_copies.append(
            push(
                gh_ref.at[rows_there, :], gh_in.at[pl.ds(128 * n, size), :],
                gh_sems.at[n], gh_sems.at[2 + n], me.far(),
            )
        )
    far[0].wait_recv()
    merge(0, 1)
    for seg_core in range(2):
        back_table[seg_core, 0], back_table[seg_core, 1] = spread(p_ref[...], seg_core, mask, True)
    probs[...] = jnp.zeros_like(probs)
    for copy in along_x:
        copy.wait_recv()

    def level(step):
        return (me.z + step + NZ) % NZ

    def part(j, half, z):
        return dot(m[j][8 * half + z], x_ref[2 * half + z // 4, z % 4], TN)

    summing, gathers, to_x, from_sibling, to_far = {}, {}, [], {}, []

    def ready(j):
        if j > 0:
            far[j].wait_recv()
            merge(j, 1)
        from_sib[j, 0].wait_recv()
        from_sib[j, 1].wait_recv()

    def reduce_step(j, t):
        for direction, half, steps in STREAMS:
            if t >= steps:
                continue
            i = INDEX[direction, half, t]
            total = part(j, half, level(direction * (steps - t)))
            if t > 0:
                summing[j, direction, half].wait_recv()
                total = total + sums_in[j][INDEX[direction, half, t - 1]].astype(F32)
            sums_out[j][i] = total.astype(BF16)
            k = 14 * j + i
            summing[j, direction, half] = push(
                sums_out[j].at[i], sums_in[j].at[i], rs_send.at[k], rs_recv.at[k], me.at_z(direction)
            )

    def gather(j, direction, half, t):
        k = 14 * j + INDEX[direction, half, t]
        block = grads[j].at[half, level(-direction * t)]
        gathers[j, direction, half, t] = push(block, block, ag_send.at[k], ag_recv.at[k], me.at_z(direction))

    def back(j, half, z):
        k = 8 * half + z
        lead = 2 * half + z // 4
        if j == 2:
            total = dot(m[0][k], grads[0][half, z]) + dot(m[1][k], grads[1][half, z])
            total = total + dot(m[2][k], grads[2][half, z])
            rows[lead, z % 4] = total.astype(BF16)
            step = (z % 4 - me.x + NX) % NX

            @pl.when(step > 0)
            def _():
                i = 4 * (step - 1) + lead
                remote(
                    rows.at[lead, z % 4], rows_in.at[step - 1, lead], rx_send.at[i], rx_recv.at[i], me.at_x(step)
                ).start()

        block = grads[j][half, z]
        full[j][k] = dot(x_ref[lead, z % 4], block, NT).astype(BF16).reshape(2, 2, 64, CHUNKS[j])

    def activate(j):
        if j == 0:
            for copy in gh_copies:
                copy.wait_recv()
        hidden = CHUNKS[j] // 2
        for half in range(2):
            pre = part(j, half, me.z)
            for direction, stream_half, steps in STREAMS:
                if stream_half == half:
                    summing[j, direction, half].wait_recv()
                    pre = pre + sums_in[j][INDEX[direction, half, steps - 1]].astype(F32)
            gate, up = pre[:hidden], pre[hidden:]
            first = 128 * me.h + 64 * j if j < 2 else 256 + 48 * me.h
            own = gh_ref[pl.ds(pl.multiple_of(first, 16), hidden), :]
            g = jnp.where(me.h == half, own.astype(F32), gh_in[64 * j : 64 * j + hidden, :].astype(F32))
            sig = 1.0 / (1.0 + jnp.exp(-gate))
            grads[j][half, me.z, 0:hidden, :] = (g * up * sig * (1.0 + gate * (1.0 - sig))).astype(BF16)
            grads[j][half, me.z, hidden : 2 * hidden, :] = (g * gate * sig).astype(BF16)
            for direction, stream_half, steps in STREAMS:
                if stream_half == half:
                    gather(j, direction, half, 0)
        back(j, 0, me.z)
        back(j, 1, me.z)

    def gather_step(j, t):
        for direction, half, steps in STREAMS:
            if t < steps:
                gathers[j, direction, half, t].wait_recv()
                if t + 1 < steps:
                    gather(j, direction, half, t + 1)
                back(j, half, level(-direction * (t + 1)))
        if t == 3:
            from_sibling[j] = push(
                full[j].at[:, :, 1 - me.c], sib_in[j], sib_send.at[j], sib_recv.at[j], me.sibling()
            )

    def weight_rows(j, half, g, raw):
        cut = slice(G * g, G * g + G)
        ours = full[j][:, half, me.c, cut, :].reshape(256, CHUNKS[j])
        theirs = sib_in[j][:, half, cut, :].reshape(256, CHUNKS[j])
        total = dot(back_table[me.c, 0], ours) + dot(back_table[me.c, 1], ours)
        total = total + (dot(back_table[1 - me.c, 0], theirs) + dot(back_table[1 - me.c, 1], theirs))
        probs[me.c] += dot(raw, ours, NT)
        probs[1 - me.c] += dot(raw, theirs, NT)
        return total.reshape(16, G, CHUNKS[j]).astype(BF16)

    def weights(j):
        from_sibling[j].wait_recv()
        for g in range(4):
            cut = slice(G * g, G * g + G)
            raw = far_in[j][:, cut, :].reshape(256, CHUNKS[j])
            gw_out[j][:, cut, :] = weight_rows(j, 1 - me.h, g, raw)
        to_far.append(push(gw_out[j], gw[j].at[me.h], out_send.at[j], out_recv.at[j], me.far()))
        for g in range(4):
            cut = slice(G * g, G * g + G)
            raw = w[j][:, cut, :].reshape(256, CHUNKS[j])
            gw[j][me.h, :, cut, :] = weight_rows(j, me.h, g, raw)

    stages = [functools.partial(reduce_step, t=t) for t in range(4)]
    stages += [activate] + [functools.partial(gather_step, t=t) for t in range(4)] + [weights]
    for tick in range(len(stages) + 2 * LEAD):
        for j in range(3):
            stage = tick - LEAD * j
            if stage == 0:
                ready(j)
            if 0 <= stage < len(stages):
                stages[stage](j)

    experts = one_hot((256, 128), G, 1, F32)
    local = jnp.zeros((32, 128), F32)
    for seg_core in range(2):
        kept = jnp.where(mask, probs[seg_core], 0.0)
        segments = jnp.where(pick(seg_core), 1.0, 0.0)
        local = local + dot(segments, dot(kept, experts, TN, HIGHEST), TN, HIGHEST)

    def sum_start(value, used, base, place, count, peer):
        ring[base + place] = value
        block = ring.at[base + place]
        return [
            push(block, block, p_send.at[used + i - 1], p_recv.at[used + i - 1], peer(i)) for i in range(1, count)
        ]

    def sum_end(copies, base, count):
        for copy in copies:
            copy.wait_recv()
        total = ring[base]
        for i in range(1, count):
            total = total + ring[base + i]
        return total

    def slice_of(y):
        row = pl.multiple_of(128 * ((y % 4) // 2), 128)
        return half_sum.at[2 * (y // 4) + y % 2, pl.ds(row, 128), :]

    def sum_x(lead):
        total = rows[lead, me.x].astype(F32)
        for step in range(1, NX):
            i = 4 * (step - 1) + lead
            block = rows_in.at[step - 1, lead]
            remote(block, block, rx_send.at[i], rx_recv.at[i], me.at_x(step)).wait_recv()
            total = total + rows_in[step - 1, lead].astype(F32)
        half_sum[lead] = total.astype(BF16)

    copies = sum_start(local, 0, 0, me.c, 2, lambda i: me.sibling())
    sum_x(0)
    sum_x(1)
    value = sum_end(copies, 0, 2)
    copies = sum_start(value, 1, 2, me.x, NX, me.at_x)
    sum_x(2)
    sum_x(3)
    along_y = []
    for i in range(1, NY):
        block = slice_of((me.y + i) % NY)
        along_y.append(push(block, slices_in.at[i - 1], ry_send.at[i - 1], ry_recv.at[i - 1], me.at_y(i)))
    value = sum_end(copies, 2, NX)
    copies = sum_start(value, 4, 6, me.y, NY, me.at_y)
    total = slice_of(me.y)[...].astype(F32)
    for i in range(NY - 1):
        along_y[i].wait_recv()
        total = total + slices_in[i].astype(F32)
    done[...] = total.astype(BF16)
    swap_start(swap, done, home, swap2)
    value = sum_end(copies, 6, NY)
    copies = sum_start(value, 11, 14, me.z, NZ, me.at_z)
    swap_wait(swap, done, home, swap2)
    gt_ref[...] = home[...].T
    gp_ref[...] = sum_end(copies, 14, NZ)[:, :16]
    for copy in to_far:
        copy.wait_recv()
    for lo in range(0, 16, 4):
        at = slice(lo, lo + 4)
        for half in range(2):
            tile = slice(128 * half, 128 * half + 128)
            first, second = gw[0][half, at], gw[1][half, at]
            gg_ref[at, :, tile] = jnp.concatenate([first[..., :64], second[..., :64]], axis=-1)
            gu_ref[at, :, tile] = jnp.concatenate([first[..., 64:], second[..., 64:]], axis=-1)
        first, second = gw[2][0, at], gw[2][1, at]
        gg_ref[at, :, 256:352] = jnp.concatenate([first[..., :48], second[..., :48]], axis=-1)
        gu_ref[at, :, 256:352] = jnp.concatenate([first[..., 48:], second[..., 48:]], axis=-1)
    for copy in sent:
        copy.wait_send()
    for step in range(1, NX):
        for lead in range(4):
            i = 4 * (step - 1) + lead
            block = rows_in.at[step - 1, lead]
            remote(block, block, rx_send.at[i], rx_recv.at[i], me.at_x(step)).wait_send()


def shape(*dims, dtype=BF16):
    return jax.ShapeDtypeStruct(dims, dtype)


def buffers(*dims):
    return pltpu.VMEM(dims, BF16)


def per_chunk(*dims):
    return [buffers(*[width if d is None else d for d in dims]) for width in CHUNKS]


def shards(tokens, grad_hidden, merge_probs, w_gate, w_up):
    out_shape = [shape(256, 128), shape(16, 64, 352), shape(16, 64, 352), shape(32, 16, dtype=F32)]
    scratch = [
        buffers(128, 256), buffers(352, 256),
        *per_chunk(16, 64, None), *per_chunk(16, 64, None), *per_chunk(2, 16, 64, None),
        buffers(2, 2, 256, 256), buffers(2, 2, 256, 256), buffers(4, 4, 256, 256), buffers(176, 256),
        pltpu.VMEM((2, 256, 256), F32), pltpu.VMEM((22, 32, 128), F32),
        *per_chunk(16, 64, None), *per_chunk(2, 16, 64, None), *per_chunk(16, 256, None),
        *per_chunk(14, None, 256), *per_chunk(14, None, 256), *per_chunk(2, 8, None, 256),
        *per_chunk(16, 2, 2, 64, None), *per_chunk(16, 2, 64, None), *per_chunk(16, 64, None),
        buffers(4, 4, 256, 256), buffers(3, 4, 256, 256), buffers(4, 256, 256), buffers(7, 128, 256),
        buffers(128, 256), buffers(128, 256),
    ]
    counts = [3, 3, 7, 7, 24, 24, 3, 3, 6, 6, 4, 42, 42, 42, 42, 3, 3, 3, 3, 12, 12, 7, 7, 18, 18]
    operands = [w_gate, w_up, tokens, grad_hidden, merge_probs]
    return pl.pallas_call(
        whole_kernel,
        out_shape=out_shape,
        in_specs=[VMEM] * len(operands),
        out_specs=[VMEM] * len(out_shape),
        scratch_shapes=scratch + [DMA((n,)) for n in counts],
        compiler_params=pltpu.CompilerParams(
            collective_id=1, has_side_effects=True, vmem_limit_bytes=56 * 1024 * 1024
        ),
        cost_estimate=pl.CostEstimate(flops=6 << 30, bytes_accessed=16 << 20, transcendentals=0),
    )(*operands)


def solution(mesh):
    return jax.shard_map(
        shards,
        mesh=mesh,
        in_specs=(
            P("dp", ("expert", "tensor")),
            P("dp", ("expert", "tensor")),
            P(),
            P(None, "dp", ("expert", "tensor")),
            P(None, "dp", ("expert", "tensor")),
        ),
        out_specs=(
            P("dp", ("expert", "tensor")),
            P(None, "dp", ("expert", "tensor")),
            P(None, "dp", ("expert", "tensor")),
            P(),
        ),
        check_vma=False,
    )
```

```python
import functools

import jax
import jax.numpy as jnp
from jax import lax
from jax.experimental import pallas as pl
from jax.experimental.pallas import tpu as pltpu
from jax.sharding import PartitionSpec as P

MESH = pl.DeviceIdType.MESH
F32, BF16 = jnp.float32, jnp.bfloat16
HIGHEST = lax.Precision.HIGHEST
VMEM = pl.BlockSpec(memory_space=pltpu.VMEM)
DMA = pltpu.SemaphoreType.DMA
NZ, NY, NX, G = 8, 8, 4, 16
TN = (((0,), (0,)), ((), ()))
NT = (((1,), (1,)), ((), ()))


class Place:
    def __init__(self):
        d = lax.axis_index("dp")
        self.h, self.z, self.c = d // 16, (d // 2) % 8, d % 2
        self.e, self.x = lax.axis_index("expert"), lax.axis_index("tensor")
        self.y = 4 * self.h + self.e

    def at(self, h=None, z=None, c=None, e=None, x=None):
        h = self.h if h is None else h
        z = self.z if z is None else z
        c = self.c if c is None else c
        return {
            "dp": h * 16 + z * 2 + c,
            "expert": self.e if e is None else e,
            "tensor": self.x if x is None else x,
        }

    def sibling(self):
        return self.at(c=1 - self.c)

    def far(self):
        return self.at(h=1 - self.h)

    def at_y(self, step):
        y = (self.y + step) % NY
        return self.at(h=y // 4, e=y % 4)

    def at_z(self, step):
        return self.at(z=(self.z + step + NZ) % NZ)

    def at_x(self, step):
        return self.at(x=(self.x + step) % NX)

    def swapped(self):
        z = 4 * (self.e % 2) + self.x
        e = 2 * (self.e // 2) + self.z // 4
        return self.at(z=z, e=e, x=self.z % 4), z == self.z


def greet(peers, swap=None):
    barrier = pltpu.get_barrier_semaphore()
    for peer in peers:
        pl.semaphore_signal(barrier, inc=1, device_id=peer, device_id_type=MESH)
    count = len(peers)
    if swap is not None:
        peer, own = swap
        count = count + jnp.where(own, 0, 1)

        @pl.when(jnp.logical_not(own))
        def _():
            pl.semaphore_signal(barrier, inc=1, device_id=peer, device_id_type=MESH)

    pl.semaphore_wait(barrier, count)


def remote(src, dst, send, recv, peer):
    return pltpu.make_async_remote_copy(
        src_ref=src, dst_ref=dst, send_sem=send, recv_sem=recv, device_id=peer, device_id_type=MESH
    )


def swap_start(swap, src, dst, sems):
    peer, own = swap

    @pl.when(own)
    def _():
        pltpu.make_async_copy(src, dst, sems.at[0]).start()

    @pl.when(jnp.logical_not(own))
    def _():
        remote(src, dst, sems.at[1], sems.at[2], peer).start()


def swap_wait(swap, src, dst, sems):
    peer, own = swap

    @pl.when(own)
    def _():
        pltpu.make_async_copy(src, dst, sems.at[0]).wait()

    @pl.when(jnp.logical_not(own))
    def _():
        remote(src, dst, sems.at[1], sems.at[2], peer).wait()


def dot(a, b, dims=(((1,), (0,)), ((), ())), precision=None):
    return lax.dot_general(a, b, dims, preferred_element_type=F32, precision=precision)


def one_hot(shape, row_div, col_div, dtype):
    rows = lax.broadcasted_iota(jnp.int32, shape, 0) // row_div
    cols = lax.broadcasted_iota(jnp.int32, shape, 1) // col_div
    return jnp.where(rows == cols, 1.0, 0.0).astype(dtype)


def diagonal():
    rows = lax.broadcasted_iota(jnp.int32, (256, 256), 0) % G
    cols = lax.broadcasted_iota(jnp.int32, (256, 256), 1) % G
    return rows == cols


def pick(core):
    rows = lax.broadcasted_iota(jnp.int32, (256, 32), 0) // G
    cols = lax.broadcasted_iota(jnp.int32, (256, 32), 1)
    return rows * 2 + core == cols


def spread(table, core, mask, transpose):
    experts = one_hot((256, 16), G, 1, BF16)
    segments = jnp.where(pick(core), 1.0, 0.0).astype(BF16)
    high = table.astype(BF16)
    low = (table - high.astype(F32)).astype(BF16)
    out = []
    for part in (high, low):
        if transpose:
            full = dot(dot(experts, part).astype(BF16), segments, NT)
        else:
            full = dot(dot(segments, part, NT).astype(BF16), experts, NT)
        out.append(jnp.where(mask, full, 0.0).astype(BF16))
    return out


STREAMS = ((1, 0, 4), (-1, 1, 4), (-1, 0, 3), (1, 1, 3))
CHUNKS = (128, 128, 96)
LEAD = 3
INDEX = {}
for _direction, _half, _steps in STREAMS:
    for _t in range(_steps):
        INDEX[_direction, _half, _t] = len(INDEX)


def whole_kernel(
    wg_in, wu_in, tok_in, grad_in, p_in,
    gt_ref, gg_ref, gu_ref, gp_ref,
    wg_ref, wu_ref, tok_ref, p_ref, load_sems, xt_ref, gh_ref, w0, w1, w2, wf0, wf1, wf2, gw0, gw1, gw2,
    forth, back_table, x_ref, gh_in, probs, ring,
    far0, far1, far2, st0, st1, st2, m0, m1, m2, so0, so1, so2, si0, si1, si2, gr0, gr1, gr2,
    full0, full1, full2, sib0, sib1, sib2, gs0, gs1, gs2,
    rows, rows_in, half_sum, slices_in, done, home,
    swap1, swap2, y_send, y_recv, x_send, x_recv, far_send, far_recv, m_send, m_recv, gh_sems,
    rs_send, rs_recv, ag_send, ag_recv, sib_send, sib_recv, out_send, out_recv,
    rx_send, rx_recv, ry_send, ry_recv, p_send, p_recv,
):
    w, w_far, gw = (w0, w1, w2), (wf0, wf1, wf2), (gw0, gw1, gw2)
    far_in, staged, m = (far0, far1, far2), (st0, st1, st2), (m0, m1, m2)
    sums_out, sums_in, grads = (so0, so1, so2), (si0, si1, si2), (gr0, gr1, gr2)
    full, sib_in, gw_out = (full0, full1, full2), (sib0, sib1, sib2), (gs0, gs1, gs2)
    loads = [
        pltpu.make_async_copy(src, dst, load_sems.at[n])
        for n, (src, dst) in enumerate(
            ((tok_in, tok_ref), (wg_in, wg_ref), (wu_in, wu_ref), (p_in, p_ref), (grad_in, gh_ref))
        )
    ]
    for load in loads:
        load.start()
    me = Place()
    swap = me.swapped()
    greet(
        [me.sibling()] + [me.at_y(i) for i in range(1, NY)] + [me.at_x(i) for i in range(1, NX)]
        + [me.at_z(i) for i in range(1, NZ)],
        swap,
    )
    sent = []

    def push(src, dst, send, recv, peer):
        copy = remote(src, dst, send, recv, peer)
        copy.start()
        sent.append(copy)
        return copy

    def slot(y, x):
        row = pl.multiple_of(128 * ((y % 4) // 2), 128)
        return x_ref.at[2 * (y // 4) + y % 2, x, pl.ds(row, 128), :]

    def push_far(j):
        return push(w_far[j], far_in[j], far_send.at[j], far_recv.at[j], me.far())

    there = x_ref.at[
        2 * me.h + me.z // 4, me.z % 4, pl.ds(pl.multiple_of(128 * (me.e // 2), 128), 128), :
    ]
    mine = slot(me.y, me.x)
    loads[0].wait()
    xt_ref[...] = tok_ref[...].T
    swap_start(swap, xt_ref, there, swap1)

    def pack(half, into):
        tile = pl.ds(pl.multiple_of(128 * half, 128), 128)
        for lo in range(0, 16, 4):
            at = slice(lo, lo + 4)
            gate, up = wg_ref[at, :, tile], wu_ref[at, :, tile]
            into[0][at] = jnp.concatenate([gate[..., :64], up[..., :64]], axis=-1)
            into[1][at] = jnp.concatenate([gate[..., 64:], up[..., 64:]], axis=-1)
            gate, up = wg_ref[at, :, 256:352], wu_ref[at, :, 256:352]
            gate = jnp.where(half == 0, gate[..., :48], gate[..., 48:])
            up = jnp.where(half == 0, up[..., :48], up[..., 48:])
            into[2][at] = jnp.concatenate([gate, up], axis=-1)

    loads[1].wait()
    loads[2].wait()
    pack(1 - me.h, w_far)
    far = [push_far(0)]
    from_sib = {}

    def merge(j, n):
        half = me.h if n == 0 else 1 - me.h
        at = pl.multiple_of(half * 128 + me.c * 64, 64)
        for other in (True, False):
            core = 1 - me.c if other else me.c
            for g in range(4):
                cut = slice(G * g, G * g + G)
                raw = w[j][:, cut, :] if n == 0 else far_in[j][:, cut, :]
                raw = raw.reshape(256, CHUNKS[j])
                out = dot(forth[core, 0], raw) + dot(forth[core, 1], raw)
                out = out.reshape(16, G, CHUNKS[j]).astype(BF16)
                if other:
                    staged[j][n, :, cut, :] = out
                else:
                    m[j][:, pl.ds(pl.multiple_of(at + G * g, G), G), :] = out
            if other:
                i = 2 * j + n
                from_sib[j, n] = push(
                    staged[j].at[n], m[j].at[:, pl.ds(at, 64), :], m_send.at[i], m_recv.at[i], me.sibling()
                )

    swap_wait(swap, xt_ref, mine, swap1)
    along_y, along_x = {}, []

    def push_x(n):
        block = slot((me.y - n + NY) % NY, me.x)
        for i in range(1, NX):
            k = (i - 1) * NY + n
            along_x.append(push(block, block, x_send.at[k], x_recv.at[k], me.at_x(i)))

    for i in (1, 7, 2, 6, 3, 5, 4):
        along_y[i] = push(mine, mine, y_send.at[i - 1], y_recv.at[i - 1], me.at_y(i))
    push_x(0)
    pack(me.h, w)
    loads[3].wait()
    mask = diagonal()
    for seg_core in range(2):
        forth[seg_core, 0], forth[seg_core, 1] = spread(p_ref[...], seg_core, mask, False)
    for n, pair in enumerate(((1, 7), (2, 6), (3, 5), (4,))):
        for i in pair:
            along_y[i].wait_recv()
            push_x(i)
        if n < 3:
            merge(n, 0)
    far += [push_far(1), push_far(2)]
    loads[4].wait()
    gh_copies = []
    for n, (base, step, size) in enumerate(((0, 128, 128), (256, 48, 48))):
        rows_there = pl.ds(pl.multiple_of(base + step * (1 - me.h), 16), size)
        gh_copies.append(
            push(
                gh_ref.at[rows_there, :], gh_in.at[pl.ds(128 * n, size), :],
                gh_sems.at[n], gh_sems.at[2 + n], me.far(),
            )
        )
    far[0].wait_recv()
    merge(0, 1)
    for seg_core in range(2):
        back_table[seg_core, 0], back_table[seg_core, 1] = spread(p_ref[...], seg_core, mask, True)
    probs[...] = jnp.zeros_like(probs)
    for copy in along_x:
        copy.wait_recv()

    def level(step):
        return (me.z + step + NZ) % NZ

    def part(j, half, z):
        return dot(m[j][8 * half + z], x_ref[2 * half + z // 4, z % 4], TN)

    summing, gathers, to_x, from_sibling, to_far = {}, {}, [], {}, []

    def ready(j):
        if j > 0:
            far[j].wait_recv()
            merge(j, 1)
        from_sib[j, 0].wait_recv()
        from_sib[j, 1].wait_recv()

    def reduce_step(j, t):
        for direction, half, steps in STREAMS:
            if t >= steps:
                continue
            i = INDEX[direction, half, t]
            total = part(j, half, level(direction * (steps - t)))
            if t > 0:
                summing[j, direction, half].wait_recv()
                total = total + sums_in[j][INDEX[direction, half, t - 1]].astype(F32)
            sums_out[j][i] = total.astype(BF16)
            k = 14 * j + i
            summing[j, direction, half] = push(
                sums_out[j].at[i], sums_in[j].at[i], rs_send.at[k], rs_recv.at[k], me.at_z(direction)
            )

    def gather(j, direction, half, t):
        k = 14 * j + INDEX[direction, half, t]
        block = grads[j].at[half, level(-direction * t)]
        gathers[j, direction, half, t] = push(block, block, ag_send.at[k], ag_recv.at[k], me.at_z(direction))

    def back(j, half, z):
        k = 8 * half + z
        lead = 2 * half + z // 4
        if j == 2:
            total = dot(m[0][k], grads[0][half, z]) + dot(m[1][k], grads[1][half, z])
            total = total + dot(m[2][k], grads[2][half, z])
            rows[lead, z % 4] = total.astype(BF16)
            step = (z % 4 - me.x + NX) % NX

            @pl.when(step > 0)
            def _():
                i = 4 * (step - 1) + lead
                remote(
                    rows.at[lead, z % 4], rows_in.at[step - 1, lead], rx_send.at[i], rx_recv.at[i], me.at_x(step)
                ).start()

        block = grads[j][half, z]
        full[j][k] = dot(x_ref[lead, z % 4], block, NT).astype(BF16).reshape(2, 2, 64, CHUNKS[j])

    def activate(j):
        if j == 0:
            for copy in gh_copies:
                copy.wait_recv()
        hidden = CHUNKS[j] // 2
        for half in range(2):
            pre = part(j, half, me.z)
            for direction, stream_half, steps in STREAMS:
                if stream_half == half:
                    summing[j, direction, half].wait_recv()
                    pre = pre + sums_in[j][INDEX[direction, half, steps - 1]].astype(F32)
            gate, up = pre[:hidden], pre[hidden:]
            first = 128 * me.h + 64 * j if j < 2 else 256 + 48 * me.h
            own = gh_ref[pl.ds(pl.multiple_of(first, 16), hidden), :]
            g = jnp.where(me.h == half, own.astype(F32), gh_in[64 * j : 64 * j + hidden, :].astype(F32))
            sig = 1.0 / (1.0 + jnp.exp(-gate))
            grads[j][half, me.z, 0:hidden, :] = (g * up * sig * (1.0 + gate * (1.0 - sig))).astype(BF16)
            grads[j][half, me.z, hidden : 2 * hidden, :] = (g * gate * sig).astype(BF16)
            for direction, stream_half, steps in STREAMS:
                if stream_half == half:
                    gather(j, direction, half, 0)
        back(j, 0, me.z)
        back(j, 1, me.z)

    def gather_step(j, t):
        for direction, half, steps in STREAMS:
            if t < steps:
                gathers[j, direction, half, t].wait_recv()
                if t + 1 < steps:
                    gather(j, direction, half, t + 1)
                back(j, half, level(-direction * (t + 1)))
        if t == 3:
            from_sibling[j] = push(
                full[j].at[:, :, 1 - me.c], sib_in[j], sib_send.at[j], sib_recv.at[j], me.sibling()
            )

    def weight_rows(j, half, g, raw):
        cut = slice(G * g, G * g + G)
        ours = full[j][:, half, me.c, cut, :].reshape(256, CHUNKS[j])
        theirs = sib_in[j][:, half, cut, :].reshape(256, CHUNKS[j])
        total = dot(back_table[me.c, 0], ours) + dot(back_table[me.c, 1], ours)
        total = total + (dot(back_table[1 - me.c, 0], theirs) + dot(back_table[1 - me.c, 1], theirs))
        probs[me.c] += dot(raw, ours, NT)
        probs[1 - me.c] += dot(raw, theirs, NT)
        return total.reshape(16, G, CHUNKS[j]).astype(BF16)

    def weights(j):
        from_sibling[j].wait_recv()
        for g in range(4):
            cut = slice(G * g, G * g + G)
            raw = far_in[j][:, cut, :].reshape(256, CHUNKS[j])
            gw_out[j][:, cut, :] = weight_rows(j, 1 - me.h, g, raw)
        to_far.append(push(gw_out[j], gw[j].at[me.h], out_send.at[j], out_recv.at[j], me.far()))
        for g in range(4):
            cut = slice(G * g, G * g + G)
            raw = w[j][:, cut, :].reshape(256, CHUNKS[j])
            gw[j][me.h, :, cut, :] = weight_rows(j, me.h, g, raw)

    stages = [functools.partial(reduce_step, t=t) for t in range(4)]
    stages += [activate] + [functools.partial(gather_step, t=t) for t in range(4)] + [weights]
    for tick in range(len(stages) + 2 * LEAD):
        for j in range(3):
            stage = tick - LEAD * j
            if stage == 0:
                ready(j)
            if 0 <= stage < len(stages):
                stages[stage](j)

    experts = one_hot((256, 128), G, 1, F32)
    local = jnp.zeros((32, 128), F32)
    for seg_core in range(2):
        kept = jnp.where(mask, probs[seg_core], 0.0)
        segments = jnp.where(pick(seg_core), 1.0, 0.0)
        local = local + dot(segments, dot(kept, experts, TN, HIGHEST), TN, HIGHEST)

    def sum_start(value, used, base, place, count, peer):
        ring[base + place] = value
        block = ring.at[base + place]
        return [
            push(block, block, p_send.at[used + i - 1], p_recv.at[used + i - 1], peer(i)) for i in range(1, count)
        ]

    def sum_end(copies, base, count):
        for copy in copies:
            copy.wait_recv()
        total = ring[base]
        for i in range(1, count):
            total = total + ring[base + i]
        return total

    def slice_of(y):
        row = pl.multiple_of(128 * ((y % 4) // 2), 128)
        return half_sum.at[2 * (y // 4) + y % 2, pl.ds(row, 128), :]

    def sum_x(lead):
        total = rows[lead, me.x].astype(F32)
        for step in range(1, NX):
            i = 4 * (step - 1) + lead
            block = rows_in.at[step - 1, lead]
            remote(block, block, rx_send.at[i], rx_recv.at[i], me.at_x(step)).wait_recv()
            total = total + rows_in[step - 1, lead].astype(F32)
        half_sum[lead] = total.astype(BF16)
        first = 4 * (lead // 2) + lead % 2
        for y in (first, first + 2):

            @pl.when(y != me.y)
            def _():
                remote(
                    slice_of(y), slices_in.at[me.y], ry_send.at[y], ry_recv.at[me.y], me.at(h=y // 4, e=y % 4)
                ).start()

    copies = sum_start(local, 0, 0, me.c, 2, lambda i: me.sibling())
    sum_x(0)
    value = sum_end(copies, 0, 2)
    copies = sum_start(value, 1, 2, me.x, NX, me.at_x)
    sum_x(1)
    value = sum_end(copies, 2, NX)
    copies = sum_start(value, 4, 6, me.y, NY, me.at_y)
    sum_x(2)
    sum_x(3)
    value = sum_end(copies, 6, NY)
    copies = sum_start(value, 11, 14, me.z, NZ, me.at_z)
    total = slice_of(me.y)[...].astype(F32)
    for i in range(1, NY):
        y = (me.y + i) % NY
        block = slices_in.at[y]
        remote(block, block, ry_send.at[y], ry_recv.at[y], me.at_y(i)).wait_recv()
        total = total + slices_in[y].astype(F32)
    done[...] = total.astype(BF16)
    swap_start(swap, done, home, swap2)
    to_far[0].wait_recv()
    to_far[1].wait_recv()
    for lo in range(0, 16, 4):
        at = slice(lo, lo + 4)
        for half in range(2):
            tile = slice(128 * half, 128 * half + 128)
            first, second = gw[0][half, at], gw[1][half, at]
            gg_ref[at, :, tile] = jnp.concatenate([first[..., :64], second[..., :64]], axis=-1)
            gu_ref[at, :, tile] = jnp.concatenate([first[..., 64:], second[..., 64:]], axis=-1)
    gp_ref[...] = sum_end(copies, 14, NZ).T[:16]
    to_far[2].wait_recv()
    for lo in range(0, 16, 4):
        at = slice(lo, lo + 4)
        first, second = gw[2][0, at], gw[2][1, at]
        gg_ref[at, :, 256:352] = jnp.concatenate([first[..., :48], second[..., :48]], axis=-1)
        gu_ref[at, :, 256:352] = jnp.concatenate([first[..., 48:], second[..., 48:]], axis=-1)
    swap_wait(swap, done, home, swap2)
    gt_ref[...] = home[...].T
    for copy in sent:
        copy.wait_send()
    for i in range(1, NY):
        y = (me.y + i) % NY
        remote(slice_of(y), slices_in.at[me.y], ry_send.at[y], ry_recv.at[me.y], me.at_y(i)).wait_send()
    for step in range(1, NX):
        for lead in range(4):
            i = 4 * (step - 1) + lead
            block = rows_in.at[step - 1, lead]
            remote(block, block, rx_send.at[i], rx_recv.at[i], me.at_x(step)).wait_send()


def shape(*dims, dtype=BF16):
    return jax.ShapeDtypeStruct(dims, dtype)


def buffers(*dims):
    return pltpu.VMEM(dims, BF16)


def per_chunk(*dims):
    return [buffers(*[width if d is None else d for d in dims]) for width in CHUNKS]


def shards(tokens, grad_hidden, merge_probs, w_gate, w_up):
    out_shape = [shape(256, 128), shape(16, 64, 352), shape(16, 64, 352), shape(16, 32, dtype=F32)]
    scratch = [
        buffers(16, 64, 352), buffers(16, 64, 352), buffers(256, 128),
        pltpu.VMEM((16, 32), F32), DMA((5,)), buffers(128, 256), buffers(352, 256),
        *per_chunk(16, 64, None), *per_chunk(16, 64, None), *per_chunk(2, 16, 64, None),
        buffers(2, 2, 256, 256), buffers(2, 2, 256, 256), buffers(4, 4, 256, 256), buffers(176, 256),
        pltpu.VMEM((2, 256, 256), F32), pltpu.VMEM((22, 32, 128), F32),
        *per_chunk(16, 64, None), *per_chunk(2, 16, 64, None), *per_chunk(16, 256, None),
        *per_chunk(14, None, 256), *per_chunk(14, None, 256), *per_chunk(2, 8, None, 256),
        *per_chunk(16, 2, 2, 64, None), *per_chunk(16, 2, 64, None), *per_chunk(16, 64, None),
        buffers(4, 4, 256, 256), buffers(3, 4, 256, 256), buffers(4, 256, 256), buffers(8, 128, 256),
        buffers(128, 256), buffers(128, 256),
    ]
    counts = [3, 3, 7, 7, 24, 24, 3, 3, 6, 6, 4, 42, 42, 42, 42, 3, 3, 3, 3, 12, 12, 8, 8, 18, 18]
    operands = [w_gate, w_up, tokens, grad_hidden.T, merge_probs.T]
    grad_tokens, grad_gate, grad_up, grad_probs = pl.pallas_call(
        whole_kernel,
        out_shape=out_shape,
        in_specs=[pl.BlockSpec(memory_space=pl.ANY)] * len(operands),
        out_specs=[VMEM] * len(out_shape),
        scratch_shapes=scratch + [DMA((n,)) for n in counts],
        compiler_params=pltpu.CompilerParams(
            collective_id=1, has_side_effects=True, vmem_limit_bytes=56 * 1024 * 1024
        ),
        cost_estimate=pl.CostEstimate(flops=6 << 30, bytes_accessed=16 << 20, transcendentals=0),
    )(*operands)
    return grad_tokens, grad_gate, grad_up, grad_probs.T


def solution(mesh):
    return jax.shard_map(
        shards,
        mesh=mesh,
        in_specs=(
            P("dp", ("expert", "tensor")),
            P("dp", ("expert", "tensor")),
            P(),
            P(None, "dp", ("expert", "tensor")),
            P(None, "dp", ("expert", "tensor")),
        ),
        out_specs=(
            P("dp", ("expert", "tensor")),
            P(None, "dp", ("expert", "tensor")),
            P(None, "dp", ("expert", "tensor")),
            P(),
        ),
        check_vma=False,
    )
```

```python
import functools

import jax
import jax.numpy as jnp
from jax import lax
from jax.experimental import pallas as pl
from jax.experimental.pallas import tpu as pltpu
from jax.sharding import PartitionSpec as P

MESH = pl.DeviceIdType.MESH
F32, BF16 = jnp.float32, jnp.bfloat16
HIGHEST = lax.Precision.HIGHEST
VMEM = pl.BlockSpec(memory_space=pltpu.VMEM)
DMA = pltpu.SemaphoreType.DMA
NZ, NY, NX, G = 8, 8, 4, 16
TN = (((0,), (0,)), ((), ()))
NT = (((1,), (1,)), ((), ()))


class Place:
    def __init__(self):
        d = lax.axis_index("dp")
        self.h, self.z, self.c = d // 16, (d // 2) % 8, d % 2
        self.e, self.x = lax.axis_index("expert"), lax.axis_index("tensor")
        self.y = 4 * self.h + self.e

    def at(self, h=None, z=None, c=None, e=None, x=None):
        h = self.h if h is None else h
        z = self.z if z is None else z
        c = self.c if c is None else c
        return {
            "dp": h * 16 + z * 2 + c,
            "expert": self.e if e is None else e,
            "tensor": self.x if x is None else x,
        }

    def sibling(self):
        return self.at(c=1 - self.c)

    def far(self):
        return self.at(h=1 - self.h)

    def at_y(self, step):
        y = (self.y + step) % NY
        return self.at(h=y // 4, e=y % 4)

    def at_z(self, step):
        return self.at(z=(self.z + step + NZ) % NZ)

    def at_x(self, step):
        return self.at(x=(self.x + step) % NX)

    def swapped(self):
        z = 4 * (self.e % 2) + self.x
        e = 2 * (self.e // 2) + self.z // 4
        return self.at(z=z, e=e, x=self.z % 4), z == self.z


def greet(peers, swap=None):
    barrier = pltpu.get_barrier_semaphore()
    for peer in peers:
        pl.semaphore_signal(barrier, inc=1, device_id=peer, device_id_type=MESH)
    count = len(peers)
    if swap is not None:
        peer, own = swap
        count = count + jnp.where(own, 0, 1)

        @pl.when(jnp.logical_not(own))
        def _():
            pl.semaphore_signal(barrier, inc=1, device_id=peer, device_id_type=MESH)

    pl.semaphore_wait(barrier, count)


def remote(src, dst, send, recv, peer):
    return pltpu.make_async_remote_copy(
        src_ref=src, dst_ref=dst, send_sem=send, recv_sem=recv, device_id=peer, device_id_type=MESH
    )


def swap_start(swap, src, dst, sems):
    peer, own = swap

    @pl.when(own)
    def _():
        pltpu.make_async_copy(src, dst, sems.at[0]).start()

    @pl.when(jnp.logical_not(own))
    def _():
        remote(src, dst, sems.at[1], sems.at[2], peer).start()


def swap_wait(swap, src, dst, sems):
    peer, own = swap

    @pl.when(own)
    def _():
        pltpu.make_async_copy(src, dst, sems.at[0]).wait()

    @pl.when(jnp.logical_not(own))
    def _():
        remote(src, dst, sems.at[1], sems.at[2], peer).wait()


def dot(a, b, dims=(((1,), (0,)), ((), ())), precision=None):
    return lax.dot_general(a, b, dims, preferred_element_type=F32, precision=precision)


def one_hot(shape, row_div, col_div, dtype):
    rows = lax.broadcasted_iota(jnp.int32, shape, 0) // row_div
    cols = lax.broadcasted_iota(jnp.int32, shape, 1) // col_div
    return jnp.where(rows == cols, 1.0, 0.0).astype(dtype)


def diagonal():
    rows = lax.broadcasted_iota(jnp.int32, (256, 256), 0) % G
    cols = lax.broadcasted_iota(jnp.int32, (256, 256), 1) % G
    return rows == cols


def pick(core):
    rows = lax.broadcasted_iota(jnp.int32, (256, 32), 0) // G
    cols = lax.broadcasted_iota(jnp.int32, (256, 32), 1)
    return rows * 2 + core == cols


def spread(table, core, mask, transpose):
    experts = one_hot((256, 16), G, 1, BF16)
    segments = jnp.where(pick(core), 1.0, 0.0).astype(BF16)
    high = table.astype(BF16)
    low = (table - high.astype(F32)).astype(BF16)
    out = []
    for part in (high, low):
        if transpose:
            full = dot(dot(experts, part).astype(BF16), segments, NT)
        else:
            full = dot(dot(segments, part, NT).astype(BF16), experts, NT)
        out.append(jnp.where(mask, full, 0.0).astype(BF16))
    return out


STREAMS = ((1, 0, 4), (-1, 1, 4), (-1, 0, 3), (1, 1, 3))
CHUNKS = (128, 128, 96)
LEAD = 3
INDEX = {}
for _direction, _half, _steps in STREAMS:
    for _t in range(_steps):
        INDEX[_direction, _half, _t] = len(INDEX)


def whole_kernel(
    wg_in, wu_in, tok_in, grad_in, p_in,
    gt_ref, gg_ref, gu_ref, gp_ref,
    wg_ref, wu_ref, tok_ref, p_ref, load_sems, xt_ref, gh_ref, w0, w1, w2, wf0, wf1, wf2, gw0, gw1, gw2,
    forth, back_table, x_ref, gh_in, probs, ring,
    far0, far1, far2, st0, st1, st2, m0, m1, m2, so0, so1, so2, si0, si1, si2, gr0, gr1, gr2,
    full0, full1, full2, sib0, sib1, sib2, gs0, gs1, gs2,
    rows, rows_in, half_sum, slices_in, done, home,
    swap1, swap2, y_send, y_recv, x_send, x_recv, far_send, far_recv, m_send, m_recv, gh_sems,
    rs_send, rs_recv, ag_send, ag_recv, sib_send, sib_recv, out_send, out_recv,
    rx_send, rx_recv, ry_send, ry_recv, p_send, p_recv,
):
    w, w_far, gw = (w0, w1, w2), (wf0, wf1, wf2), (gw0, gw1, gw2)
    far_in, staged, m = (far0, far1, far2), (st0, st1, st2), (m0, m1, m2)
    sums_out, sums_in, grads = (so0, so1, so2), (si0, si1, si2), (gr0, gr1, gr2)
    full, sib_in, gw_out = (full0, full1, full2), (sib0, sib1, sib2), (gs0, gs1, gs2)
    loads = [
        pltpu.make_async_copy(src, dst, load_sems.at[n])
        for n, (src, dst) in enumerate(
            ((tok_in, tok_ref), (wg_in, wg_ref), (wu_in, wu_ref), (p_in, p_ref), (grad_in, gh_ref))
        )
    ]
    for load in loads:
        load.start()
    me = Place()
    swap = me.swapped()
    greet(
        [me.sibling()] + [me.at_y(i) for i in range(1, NY)] + [me.at_x(i) for i in range(1, NX)]
        + [me.at_z(i) for i in range(1, NZ)],
        swap,
    )
    sent = []

    def push(src, dst, send, recv, peer):
        copy = remote(src, dst, send, recv, peer)
        copy.start()
        sent.append(copy)
        return copy

    def slot(y, x):
        row = pl.multiple_of(128 * ((y % 4) // 2), 128)
        return x_ref.at[2 * (y // 4) + y % 2, x, pl.ds(row, 128), :]

    def push_far(j):
        return push(w_far[j], far_in[j], far_send.at[j], far_recv.at[j], me.far())

    there = x_ref.at[
        2 * me.h + me.z // 4, me.z % 4, pl.ds(pl.multiple_of(128 * (me.e // 2), 128), 128), :
    ]
    mine = slot(me.y, me.x)
    loads[0].wait()
    xt_ref[...] = tok_ref[...].T
    swap_start(swap, xt_ref, there, swap1)

    def pack(half, into):
        tile = pl.ds(pl.multiple_of(128 * half, 128), 128)
        for lo in range(0, 16, 4):
            at = slice(lo, lo + 4)
            gate, up = wg_ref[at, :, tile], wu_ref[at, :, tile]
            into[0][at] = jnp.concatenate([gate[..., :64], up[..., :64]], axis=-1)
            into[1][at] = jnp.concatenate([gate[..., 64:], up[..., 64:]], axis=-1)
            gate, up = wg_ref[at, :, 256:352], wu_ref[at, :, 256:352]
            gate = jnp.where(half == 0, gate[..., :48], gate[..., 48:])
            up = jnp.where(half == 0, up[..., :48], up[..., 48:])
            into[2][at] = jnp.concatenate([gate, up], axis=-1)

    loads[1].wait()
    loads[2].wait()
    pack(1 - me.h, w_far)
    far = [push_far(0)]
    from_sib = {}

    def merge(j, n):
        half = me.h if n == 0 else 1 - me.h
        at = pl.multiple_of(half * 128 + me.c * 64, 64)
        for other in (True, False):
            core = 1 - me.c if other else me.c
            for g in range(4):
                cut = slice(G * g, G * g + G)
                raw = w[j][:, cut, :] if n == 0 else far_in[j][:, cut, :]
                raw = raw.reshape(256, CHUNKS[j])
                out = dot(forth[core, 0], raw) + dot(forth[core, 1], raw)
                out = out.reshape(16, G, CHUNKS[j]).astype(BF16)
                if other:
                    staged[j][n, :, cut, :] = out
                else:
                    m[j][:, pl.ds(pl.multiple_of(at + G * g, G), G), :] = out
            if other:
                i = 2 * j + n
                from_sib[j, n] = push(
                    staged[j].at[n], m[j].at[:, pl.ds(at, 64), :], m_send.at[i], m_recv.at[i], me.sibling()
                )

    swap_wait(swap, xt_ref, mine, swap1)
    along_y, along_x = {}, {}

    def push_y(n, ahead):
        home = me.y - (n - 1) if ahead > 0 else me.y + (7 - n)
        block = slot((home + NY) % NY, me.x)
        along_y[n] = push(block, block, y_send.at[n - 1], y_recv.at[n - 1], me.at_y(ahead % NY))

    def push_x(n):
        block = slot((me.y - n + NY) % NY, me.x)
        for i in (1, 3):
            k = (i - 1) * NY + n
            along_x[i, n] = push(block, block, x_send.at[k], x_recv.at[k], me.at_x(i))

    def pass_x(n):
        i = 1 if n in (0, 7, 6, 5) else 3
        along_x[i, n].wait_recv()
        block = slot((me.y - n + NY) % NY, (me.x + 4 - i) % NX)
        k = NY + n
        along_x[2, n] = push(block, block, x_send.at[k], x_recv.at[k], me.at_x(i))

    push_y(1, 1)
    push_y(7, -1)
    push_x(0)
    pack(me.h, w)
    loads[3].wait()
    mask = diagonal()
    for seg_core in range(2):
        forth[seg_core, 0], forth[seg_core, 1] = spread(p_ref[...], seg_core, mask, False)
    for n, pair in enumerate(((1, 7), (2, 6), (3, 5), (4,))):
        for i in pair:
            along_y[i].wait_recv()
            if i < 4:
                push_y(i + 1, 1)
            elif i > 5:
                push_y(i - 1, -1)
            push_x(i)
        if n < 3:
            merge(n, 0)
    for n in (0, 1, 7, 2, 6, 3, 5, 4):
        pass_x(n)
    far += [push_far(1), push_far(2)]
    loads[4].wait()
    gh_copies = []
    for n, (base, step, size) in enumerate(((0, 128, 128), (256, 48, 48))):
        rows_there = pl.ds(pl.multiple_of(base + step * (1 - me.h), 16), size)
        gh_copies.append(
            push(
                gh_ref.at[rows_there, :], gh_in.at[pl.ds(128 * n, size), :],
                gh_sems.at[n], gh_sems.at[2 + n], me.far(),
            )
        )
    far[0].wait_recv()
    merge(0, 1)
    for seg_core in range(2):
        back_table[seg_core, 0], back_table[seg_core, 1] = spread(p_ref[...], seg_core, mask, True)
    probs[...] = jnp.zeros_like(probs)
    for n in range(NY):
        for i in (2, 3 if n in (0, 7, 6, 5) else 1):
            along_x[i, n].wait_recv()

    def level(step):
        return (me.z + step + NZ) % NZ

    def part(j, half, z):
        return dot(m[j][8 * half + z], x_ref[2 * half + z // 4, z % 4], TN)

    summing, gathers, to_x, from_sibling, to_far = {}, {}, [], {}, []

    def ready(j):
        if j > 0:
            far[j].wait_recv()
            merge(j, 1)
        from_sib[j, 0].wait_recv()
        from_sib[j, 1].wait_recv()

    def reduce_step(j, t):
        for direction, half, steps in STREAMS:
            if t >= steps:
                continue
            i = INDEX[direction, half, t]
            total = part(j, half, level(direction * (steps - t)))
            if t > 0:
                summing[j, direction, half].wait_recv()
                total = total + sums_in[j][INDEX[direction, half, t - 1]].astype(F32)
            sums_out[j][i] = total.astype(BF16)
            k = 14 * j + i
            summing[j, direction, half] = push(
                sums_out[j].at[i], sums_in[j].at[i], rs_send.at[k], rs_recv.at[k], me.at_z(direction)
            )

    def gather(j, direction, half, t):
        k = 14 * j + INDEX[direction, half, t]
        block = grads[j].at[half, level(-direction * t)]
        gathers[j, direction, half, t] = push(block, block, ag_send.at[k], ag_recv.at[k], me.at_z(direction))

    def back(j, half, z):
        k = 8 * half + z
        lead = 2 * half + z // 4
        if j == 2:
            total = dot(m[0][k], grads[0][half, z]) + dot(m[1][k], grads[1][half, z])
            total = total + dot(m[2][k], grads[2][half, z])
            rows[lead, z % 4] = total.astype(BF16)
            step = (z % 4 - me.x + NX) % NX

            @pl.when(step > 0)
            def _():
                i = 4 * (step - 1) + lead
                remote(
                    rows.at[lead, z % 4], rows_in.at[step - 1, lead], rx_send.at[i], rx_recv.at[i], me.at_x(step)
                ).start()

        block = grads[j][half, z]
        full[j][k] = dot(x_ref[lead, z % 4], block, NT).astype(BF16).reshape(2, 2, 64, CHUNKS[j])

    def activate(j):
        if j == 0:
            for copy in gh_copies:
                copy.wait_recv()
        hidden = CHUNKS[j] // 2
        for half in range(2):
            pre = part(j, half, me.z)
            for direction, stream_half, steps in STREAMS:
                if stream_half == half:
                    summing[j, direction, half].wait_recv()
                    pre = pre + sums_in[j][INDEX[direction, half, steps - 1]].astype(F32)
            gate, up = pre[:hidden], pre[hidden:]
            first = 128 * me.h + 64 * j if j < 2 else 256 + 48 * me.h
            own = gh_ref[pl.ds(pl.multiple_of(first, 16), hidden), :]
            g = jnp.where(me.h == half, own.astype(F32), gh_in[64 * j : 64 * j + hidden, :].astype(F32))
            sig = 1.0 / (1.0 + jnp.exp(-gate))
            grads[j][half, me.z, 0:hidden, :] = (g * up * sig * (1.0 + gate * (1.0 - sig))).astype(BF16)
            grads[j][half, me.z, hidden : 2 * hidden, :] = (g * gate * sig).astype(BF16)
            for direction, stream_half, steps in STREAMS:
                if stream_half == half:
                    gather(j, direction, half, 0)
        back(j, 0, me.z)
        back(j, 1, me.z)

    def gather_step(j, t):
        for direction, half, steps in STREAMS:
            if t < steps:
                gathers[j, direction, half, t].wait_recv()
                if t + 1 < steps:
                    gather(j, direction, half, t + 1)
                back(j, half, level(-direction * (t + 1)))
        if t == 3:
            from_sibling[j] = push(
                full[j].at[:, :, 1 - me.c], sib_in[j], sib_send.at[j], sib_recv.at[j], me.sibling()
            )

    def weight_rows(j, half, g, raw):
        cut = slice(G * g, G * g + G)
        ours = full[j][:, half, me.c, cut, :].reshape(256, CHUNKS[j])
        theirs = sib_in[j][:, half, cut, :].reshape(256, CHUNKS[j])
        total = dot(back_table[me.c, 0], ours) + dot(back_table[me.c, 1], ours)
        total = total + (dot(back_table[1 - me.c, 0], theirs) + dot(back_table[1 - me.c, 1], theirs))
        probs[me.c] += dot(raw, ours, NT)
        probs[1 - me.c] += dot(raw, theirs, NT)
        return total.reshape(16, G, CHUNKS[j]).astype(BF16)

    def weights(j):
        from_sibling[j].wait_recv()
        for g in range(4):
            cut = slice(G * g, G * g + G)
            raw = far_in[j][:, cut, :].reshape(256, CHUNKS[j])
            gw_out[j][:, cut, :] = weight_rows(j, 1 - me.h, g, raw)
        to_far.append(push(gw_out[j], gw[j].at[me.h], out_send.at[j], out_recv.at[j], me.far()))
        for g in range(4):
            cut = slice(G * g, G * g + G)
            raw = w[j][:, cut, :].reshape(256, CHUNKS[j])
            gw[j][me.h, :, cut, :] = weight_rows(j, me.h, g, raw)

    stages = [functools.partial(reduce_step, t=t) for t in range(4)]
    stages += [activate] + [functools.partial(gather_step, t=t) for t in range(4)] + [weights]
    for tick in range(len(stages) + 2 * LEAD):
        for j in range(3):
            stage = tick - LEAD * j
            if stage == 0:
                ready(j)
            if 0 <= stage < len(stages):
                stages[stage](j)

    experts = one_hot((256, 128), G, 1, F32)
    local = jnp.zeros((32, 128), F32)
    for seg_core in range(2):
        kept = jnp.where(mask, probs[seg_core], 0.0)
        segments = jnp.where(pick(seg_core), 1.0, 0.0)
        local = local + dot(segments, dot(kept, experts, TN, HIGHEST), TN, HIGHEST)

    def sum_start(value, used, base, place, count, peer):
        ring[base + place] = value
        block = ring.at[base + place]
        return [
            push(block, block, p_send.at[used + i - 1], p_recv.at[used + i - 1], peer(i)) for i in range(1, count)
        ]

    def sum_end(copies, base, count):
        for copy in copies:
            copy.wait_recv()
        total = ring[base]
        for i in range(1, count):
            total = total + ring[base + i]
        return total

    def slice_of(y):
        row = pl.multiple_of(128 * ((y % 4) // 2), 128)
        return half_sum.at[2 * (y // 4) + y % 2, pl.ds(row, 128), :]

    def sum_x(lead):
        total = rows[lead, me.x].astype(F32)
        for step in range(1, NX):
            i = 4 * (step - 1) + lead
            block = rows_in.at[step - 1, lead]
            remote(block, block, rx_send.at[i], rx_recv.at[i], me.at_x(step)).wait_recv()
            total = total + rows_in[step - 1, lead].astype(F32)
        half_sum[lead] = total.astype(BF16)
        first = 4 * (lead // 2) + lead % 2
        for y in (first, first + 2):

            @pl.when(y != me.y)
            def _():
                remote(
                    slice_of(y), slices_in.at[me.y], ry_send.at[y], ry_recv.at[me.y], me.at(h=y // 4, e=y % 4)
                ).start()

    copies = sum_start(local, 0, 0, me.c, 2, lambda i: me.sibling())
    sum_x(0)
    value = sum_end(copies, 0, 2)
    copies = sum_start(value, 1, 2, me.x, NX, me.at_x)
    sum_x(1)
    value = sum_end(copies, 2, NX)
    copies = sum_start(value, 4, 6, me.y, NY, me.at_y)
    sum_x(2)
    sum_x(3)
    value = sum_end(copies, 6, NY)
    copies = sum_start(value, 11, 14, me.z, NZ, me.at_z)
    total = slice_of(me.y)[...].astype(F32)
    for i in range(1, NY):
        y = (me.y + i) % NY
        block = slices_in.at[y]
        remote(block, block, ry_send.at[y], ry_recv.at[y], me.at_y(i)).wait_recv()
        total = total + slices_in[y].astype(F32)
    done[...] = total.astype(BF16)
    swap_start(swap, done, home, swap2)
    to_far[0].wait_recv()
    to_far[1].wait_recv()
    for lo in range(0, 16, 4):
        at = slice(lo, lo + 4)
        for half in range(2):
            tile = slice(128 * half, 128 * half + 128)
            first, second = gw[0][half, at], gw[1][half, at]
            gg_ref[at, :, tile] = jnp.concatenate([first[..., :64], second[..., :64]], axis=-1)
            gu_ref[at, :, tile] = jnp.concatenate([first[..., 64:], second[..., 64:]], axis=-1)
    gp_ref[...] = sum_end(copies, 14, NZ).T[:16]
    to_far[2].wait_recv()
    for lo in range(0, 16, 4):
        at = slice(lo, lo + 4)
        first, second = gw[2][0, at], gw[2][1, at]
        gg_ref[at, :, 256:352] = jnp.concatenate([first[..., :48], second[..., :48]], axis=-1)
        gu_ref[at, :, 256:352] = jnp.concatenate([first[..., 48:], second[..., 48:]], axis=-1)
    swap_wait(swap, done, home, swap2)
    gt_ref[...] = home[...].T
    for copy in sent:
        copy.wait_send()
    for i in range(1, NY):
        y = (me.y + i) % NY
        remote(slice_of(y), slices_in.at[me.y], ry_send.at[y], ry_recv.at[me.y], me.at_y(i)).wait_send()
    for step in range(1, NX):
        for lead in range(4):
            i = 4 * (step - 1) + lead
            block = rows_in.at[step - 1, lead]
            remote(block, block, rx_send.at[i], rx_recv.at[i], me.at_x(step)).wait_send()


def shape(*dims, dtype=BF16):
    return jax.ShapeDtypeStruct(dims, dtype)


def buffers(*dims):
    return pltpu.VMEM(dims, BF16)


def per_chunk(*dims):
    return [buffers(*[width if d is None else d for d in dims]) for width in CHUNKS]


def shards(tokens, grad_hidden, merge_probs, w_gate, w_up):
    out_shape = [shape(256, 128), shape(16, 64, 352), shape(16, 64, 352), shape(16, 32, dtype=F32)]
    scratch = [
        buffers(16, 64, 352), buffers(16, 64, 352), buffers(256, 128),
        pltpu.VMEM((16, 32), F32), DMA((5,)), buffers(128, 256), buffers(352, 256),
        *per_chunk(16, 64, None), *per_chunk(16, 64, None), *per_chunk(2, 16, 64, None),
        buffers(2, 2, 256, 256), buffers(2, 2, 256, 256), buffers(4, 4, 256, 256), buffers(176, 256),
        pltpu.VMEM((2, 256, 256), F32), pltpu.VMEM((22, 32, 128), F32),
        *per_chunk(16, 64, None), *per_chunk(2, 16, 64, None), *per_chunk(16, 256, None),
        *per_chunk(14, None, 256), *per_chunk(14, None, 256), *per_chunk(2, 8, None, 256),
        *per_chunk(16, 2, 2, 64, None), *per_chunk(16, 2, 64, None), *per_chunk(16, 64, None),
        buffers(4, 4, 256, 256), buffers(3, 4, 256, 256), buffers(4, 256, 256), buffers(8, 128, 256),
        buffers(128, 256), buffers(128, 256),
    ]
    counts = [3, 3, 7, 7, 24, 24, 3, 3, 6, 6, 4, 42, 42, 42, 42, 3, 3, 3, 3, 12, 12, 8, 8, 18, 18]
    operands = [w_gate, w_up, tokens, grad_hidden.T, merge_probs.T]
    grad_tokens, grad_gate, grad_up, grad_probs = pl.pallas_call(
        whole_kernel,
        out_shape=out_shape,
        in_specs=[pl.BlockSpec(memory_space=pl.ANY)] * len(operands),
        out_specs=[VMEM] * len(out_shape),
        scratch_shapes=scratch + [DMA((n,)) for n in counts],
        compiler_params=pltpu.CompilerParams(
            collective_id=1, has_side_effects=True, vmem_limit_bytes=56 * 1024 * 1024
        ),
        cost_estimate=pl.CostEstimate(flops=6 << 30, bytes_accessed=16 << 20, transcendentals=0),
    )(*operands)
    return grad_tokens, grad_gate, grad_up, grad_probs.T


def solution(mesh):
    return jax.shard_map(
        shards,
        mesh=mesh,
        in_specs=(
            P("dp", ("expert", "tensor")),
            P("dp", ("expert", "tensor")),
            P(),
            P(None, "dp", ("expert", "tensor")),
            P(None, "dp", ("expert", "tensor")),
        ),
        out_specs=(
            P("dp", ("expert", "tensor")),
            P(None, "dp", ("expert", "tensor")),
            P(None, "dp", ("expert", "tensor")),
            P(),
        ),
        check_vma=False,
    )
```

```python
import functools

import jax
import jax.numpy as jnp
from jax import lax
from jax.experimental import pallas as pl
from jax.experimental.pallas import tpu as pltpu
from jax.sharding import PartitionSpec as P

MESH = pl.DeviceIdType.MESH
F32, BF16 = jnp.float32, jnp.bfloat16
HIGHEST = lax.Precision.HIGHEST
VMEM = pl.BlockSpec(memory_space=pltpu.VMEM)
DMA = pltpu.SemaphoreType.DMA
NZ, NY, NX, G = 8, 8, 4, 16
TN = (((0,), (0,)), ((), ()))
NT = (((1,), (1,)), ((), ()))


class Place:
    def __init__(self):
        d = lax.axis_index("dp")
        self.h, self.z, self.c = d // 16, (d // 2) % 8, d % 2
        self.e, self.x = lax.axis_index("expert"), lax.axis_index("tensor")
        self.y = 4 * self.h + self.e

    def at(self, h=None, z=None, c=None, e=None, x=None):
        h = self.h if h is None else h
        z = self.z if z is None else z
        c = self.c if c is None else c
        return {
            "dp": h * 16 + z * 2 + c,
            "expert": self.e if e is None else e,
            "tensor": self.x if x is None else x,
        }

    def sibling(self):
        return self.at(c=1 - self.c)

    def far(self):
        return self.at(h=1 - self.h)

    def at_y(self, step):
        y = (self.y + step) % NY
        return self.at(h=y // 4, e=y % 4)

    def at_z(self, step):
        return self.at(z=(self.z + step + NZ) % NZ)

    def at_x(self, step):
        return self.at(x=(self.x + step) % NX)

    def swapped(self):
        z = 4 * (self.e % 2) + self.x
        e = 2 * (self.e // 2) + self.z // 4
        return self.at(z=z, e=e, x=self.z % 4), z == self.z


def greet(peers, swap=None):
    barrier = pltpu.get_barrier_semaphore()
    for peer in peers:
        pl.semaphore_signal(barrier, inc=1, device_id=peer, device_id_type=MESH)
    count = len(peers)
    if swap is not None:
        peer, own = swap
        count = count + jnp.where(own, 0, 1)

        @pl.when(jnp.logical_not(own))
        def _():
            pl.semaphore_signal(barrier, inc=1, device_id=peer, device_id_type=MESH)

    pl.semaphore_wait(barrier, count)


def remote(src, dst, send, recv, peer):
    return pltpu.make_async_remote_copy(
        src_ref=src, dst_ref=dst, send_sem=send, recv_sem=recv, device_id=peer, device_id_type=MESH
    )


def swap_start(swap, src, dst, sems):
    peer, own = swap

    @pl.when(own)
    def _():
        pltpu.make_async_copy(src, dst, sems.at[0]).start()

    @pl.when(jnp.logical_not(own))
    def _():
        remote(src, dst, sems.at[1], sems.at[2], peer).start()


def swap_wait(swap, src, dst, sems):
    peer, own = swap

    @pl.when(own)
    def _():
        pltpu.make_async_copy(src, dst, sems.at[0]).wait()

    @pl.when(jnp.logical_not(own))
    def _():
        remote(src, dst, sems.at[1], sems.at[2], peer).wait()


def dot(a, b, dims=(((1,), (0,)), ((), ())), precision=None):
    return lax.dot_general(a, b, dims, preferred_element_type=F32, precision=precision)


def one_hot(shape, row_div, col_div, dtype):
    rows = lax.broadcasted_iota(jnp.int32, shape, 0) // row_div
    cols = lax.broadcasted_iota(jnp.int32, shape, 1) // col_div
    return jnp.where(rows == cols, 1.0, 0.0).astype(dtype)


def diagonal():
    rows = lax.broadcasted_iota(jnp.int32, (256, 256), 0) % G
    cols = lax.broadcasted_iota(jnp.int32, (256, 256), 1) % G
    return rows == cols


def pick(core):
    rows = lax.broadcasted_iota(jnp.int32, (256, 32), 0) // G
    cols = lax.broadcasted_iota(jnp.int32, (256, 32), 1)
    return rows * 2 + core == cols


def spread(table, core, mask, transpose):
    experts = one_hot((256, 16), G, 1, BF16)
    segments = jnp.where(pick(core), 1.0, 0.0).astype(BF16)
    high = table.astype(BF16)
    low = (table - high.astype(F32)).astype(BF16)
    out = []
    for part in (high, low):
        if transpose:
            full = dot(dot(experts, part).astype(BF16), segments, NT)
        else:
            full = dot(dot(segments, part, NT).astype(BF16), experts, NT)
        out.append(jnp.where(mask, full, 0.0).astype(BF16))
    return out


STREAMS = ((1, 0, 4), (-1, 1, 4), (-1, 0, 3), (1, 1, 3))
CHUNKS = (128, 128, 96)
LEAD = 3
INDEX = {}
for _direction, _half, _steps in STREAMS:
    for _t in range(_steps):
        INDEX[_direction, _half, _t] = len(INDEX)


def whole_kernel(
    wg_in, wu_in, tok_in, grad_in, p_in,
    gt_ref, gg_ref, gu_ref, gp_ref,
    wg_ref, wu_ref, tok_ref, p_ref, load_sems, xt_ref, gh_ref, w0, w1, w2, wf0, wf1, wf2, gw0, gw1, gw2,
    forth, back_table, x_ref, gh_in, probs, ring,
    far0, far1, far2, st0, st1, st2, m0, m1, m2, so0, so1, so2, si0, si1, si2, gr0, gr1, gr2,
    full0, full1, full2, sib0, sib1, sib2, gs0, gs1, gs2,
    rows, rows_in, half_sum, slices_in, done, home,
    swap1, swap2, y_send, y_recv, x_send, x_recv, far_send, far_recv, m_send, m_recv, gh_sems,
    rs_send, rs_recv, ag_send, ag_recv, sib_send, sib_recv, out_send, out_recv,
    rx_send, rx_recv, ry_send, ry_recv, p_send, p_recv,
):
    w, w_far, gw = (w0, w1, w2), (wf0, wf1, wf2), (gw0, gw1, gw2)
    far_in, staged, m = (far0, far1, far2), (st0, st1, st2), (m0, m1, m2)
    sums_out, sums_in, grads = (so0, so1, so2), (si0, si1, si2), (gr0, gr1, gr2)
    full, sib_in, gw_out = (full0, full1, full2), (sib0, sib1, sib2), (gs0, gs1, gs2)
    loads = [
        pltpu.make_async_copy(src, dst, load_sems.at[n])
        for n, (src, dst) in enumerate(
            ((tok_in, tok_ref), (wg_in, wg_ref), (wu_in, wu_ref), (p_in, p_ref), (grad_in, gh_ref))
        )
    ]
    for load in loads:
        load.start()
    me = Place()
    swap = me.swapped()
    greet(
        [me.sibling()] + [me.at_y(i) for i in range(1, NY)] + [me.at_x(i) for i in range(1, NX)]
        + [me.at_z(i) for i in range(1, NZ)],
        swap,
    )
    sent = []

    def push(src, dst, send, recv, peer):
        copy = remote(src, dst, send, recv, peer)
        copy.start()
        sent.append(copy)
        return copy

    def slot(y, x):
        row = pl.multiple_of(128 * ((y % 4) // 2), 128)
        return x_ref.at[2 * (y // 4) + y % 2, x, pl.ds(row, 128), :]

    def push_far(j):
        return push(w_far[j], far_in[j], far_send.at[j], far_recv.at[j], me.far())

    there = x_ref.at[
        2 * me.h + me.z // 4, me.z % 4, pl.ds(pl.multiple_of(128 * (me.e // 2), 128), 128), :
    ]
    mine = slot(me.y, me.x)
    loads[0].wait()
    xt_ref[...] = tok_ref[...].T
    swap_start(swap, xt_ref, there, swap1)

    def pack(half, into):
        tile = pl.ds(pl.multiple_of(128 * half, 128), 128)
        for lo in range(0, 16, 4):
            at = slice(lo, lo + 4)
            gate, up = wg_ref[at, :, tile], wu_ref[at, :, tile]
            into[0][at] = jnp.concatenate([gate[..., :64], up[..., :64]], axis=-1)
            into[1][at] = jnp.concatenate([gate[..., 64:], up[..., 64:]], axis=-1)
            gate, up = wg_ref[at, :, 256:352], wu_ref[at, :, 256:352]
            gate = jnp.where(half == 0, gate[..., :48], gate[..., 48:])
            up = jnp.where(half == 0, up[..., :48], up[..., 48:])
            into[2][at] = jnp.concatenate([gate, up], axis=-1)

    loads[1].wait()
    loads[2].wait()
    pack(1 - me.h, w_far)
    far = [push_far(0)]
    from_sib = {}

    def merge(j, n):
        half = me.h if n == 0 else 1 - me.h
        at = pl.multiple_of(half * 128 + me.c * 64, 64)
        for other in (True, False):
            core = 1 - me.c if other else me.c
            for g in range(4):
                cut = slice(G * g, G * g + G)
                raw = w[j][:, cut, :] if n == 0 else far_in[j][:, cut, :]
                raw = raw.reshape(256, CHUNKS[j])
                out = dot(forth[core, 0], raw) + dot(forth[core, 1], raw)
                out = out.reshape(16, G, CHUNKS[j]).astype(BF16)
                if other:
                    staged[j][n, :, cut, :] = out
                else:
                    m[j][:, pl.ds(pl.multiple_of(at + G * g, G), G), :] = out
            if other:
                i = 2 * j + n
                from_sib[j, n] = push(
                    staged[j].at[n], m[j].at[:, pl.ds(at, 64), :], m_send.at[i], m_recv.at[i], me.sibling()
                )

    swap_wait(swap, xt_ref, mine, swap1)
    along_y, along_x = {}, {}

    def push_y(n, ahead):
        home = me.y - (n - 1) if ahead > 0 else me.y + (7 - n)
        block = slot((home + NY) % NY, me.x)
        along_y[n] = push(block, block, y_send.at[n - 1], y_recv.at[n - 1], me.at_y(ahead % NY))

    def push_x(n):
        block = slot((me.y - n + NY) % NY, me.x)
        for i in (1, 3):
            k = (i - 1) * NY + n
            along_x[i, n] = push(block, block, x_send.at[k], x_recv.at[k], me.at_x(i))

    def pass_x(n):
        i = 1 if n in (0, 7, 6, 5) else 3
        along_x[i, n].wait_recv()
        block = slot((me.y - n + NY) % NY, (me.x + 4 - i) % NX)
        k = NY + n
        along_x[2, n] = push(block, block, x_send.at[k], x_recv.at[k], me.at_x(i))

    push_y(1, 1)
    push_y(7, -1)
    push_x(0)
    pack(me.h, w)
    loads[3].wait()
    mask = diagonal()
    for seg_core in range(2):
        forth[seg_core, 0], forth[seg_core, 1] = spread(p_ref[...], seg_core, mask, False)
    for n, pair in enumerate(((1, 7), (2, 6), (3, 5), (4,))):
        for i in pair:
            along_y[i].wait_recv()
            if i < 4:
                push_y(i + 1, 1)
            elif i > 5:
                push_y(i - 1, -1)
            push_x(i)
        if n < 3:
            merge(n, 0)
    for n in (0, 1, 7, 2, 6, 3, 5, 4):
        pass_x(n)
    far.append(push_far(1))
    loads[4].wait()
    gh_copies = []
    for n, (base, step, size) in enumerate(((0, 128, 128), (256, 48, 48))):
        rows_there = pl.ds(pl.multiple_of(base + step * (1 - me.h), 16), size)
        gh_copies.append(
            push(
                gh_ref.at[rows_there, :], gh_in.at[pl.ds(128 * n, size), :],
                gh_sems.at[n], gh_sems.at[2 + n], me.far(),
            )
        )
    far[0].wait_recv()
    merge(0, 1)
    for seg_core in range(2):
        back_table[seg_core, 0], back_table[seg_core, 1] = spread(p_ref[...], seg_core, mask, True)
    probs[...] = jnp.zeros_like(probs)
    for n in range(NY):
        for i in (2, 3 if n in (0, 7, 6, 5) else 1):
            along_x[i, n].wait_recv()

    def level(step):
        return (me.z + step + NZ) % NZ

    def part(j, half, z):
        return dot(m[j][8 * half + z], x_ref[2 * half + z // 4, z % 4], TN)

    summing, gathers, to_x, from_sibling, to_far = {}, {}, [], {}, []

    def ready(j):
        if j > 0:
            far[j].wait_recv()
            if j == 1:
                far.append(push_far(2))
            merge(j, 1)
        from_sib[j, 0].wait_recv()
        from_sib[j, 1].wait_recv()

    def reduce_step(j, t):
        for direction, half, steps in STREAMS:
            if t >= steps:
                continue
            i = INDEX[direction, half, t]
            total = part(j, half, level(direction * (steps - t)))
            if t > 0:
                summing[j, direction, half].wait_recv()
                total = total + sums_in[j][INDEX[direction, half, t - 1]].astype(F32)
            sums_out[j][i] = total.astype(BF16)
            k = 14 * j + i
            summing[j, direction, half] = push(
                sums_out[j].at[i], sums_in[j].at[i], rs_send.at[k], rs_recv.at[k], me.at_z(direction)
            )

    def gather(j, direction, half, t):
        k = 14 * j + INDEX[direction, half, t]
        block = grads[j].at[half, level(-direction * t)]
        gathers[j, direction, half, t] = push(block, block, ag_send.at[k], ag_recv.at[k], me.at_z(direction))

    def back(j, half, z):
        k = 8 * half + z
        lead = 2 * half + z // 4
        if j == 2:
            total = dot(m[0][k], grads[0][half, z]) + dot(m[1][k], grads[1][half, z])
            total = total + dot(m[2][k], grads[2][half, z])
            rows[lead, z % 4] = total.astype(BF16)
            step = (z % 4 - me.x + NX) % NX

            @pl.when(step > 0)
            def _():
                i = 4 * (step - 1) + lead
                remote(
                    rows.at[lead, z % 4], rows_in.at[step - 1, lead], rx_send.at[i], rx_recv.at[i], me.at_x(step)
                ).start()

        block = grads[j][half, z]
        full[j][k] = dot(x_ref[lead, z % 4], block, NT).astype(BF16).reshape(2, 2, 64, CHUNKS[j])

    def activate(j):
        if j == 0:
            for copy in gh_copies:
                copy.wait_recv()
        hidden = CHUNKS[j] // 2
        for half in range(2):
            pre = part(j, half, me.z)
            for direction, stream_half, steps in STREAMS:
                if stream_half == half:
                    summing[j, direction, half].wait_recv()
                    pre = pre + sums_in[j][INDEX[direction, half, steps - 1]].astype(F32)
            gate, up = pre[:hidden], pre[hidden:]
            first = 128 * me.h + 64 * j if j < 2 else 256 + 48 * me.h
            own = gh_ref[pl.ds(pl.multiple_of(first, 16), hidden), :]
            g = jnp.where(me.h == half, own.astype(F32), gh_in[64 * j : 64 * j + hidden, :].astype(F32))
            sig = 1.0 / (1.0 + jnp.exp(-gate))
            grads[j][half, me.z, 0:hidden, :] = (g * up * sig * (1.0 + gate * (1.0 - sig))).astype(BF16)
            grads[j][half, me.z, hidden : 2 * hidden, :] = (g * gate * sig).astype(BF16)
            for direction, stream_half, steps in STREAMS:
                if stream_half == half:
                    gather(j, direction, half, 0)
        back(j, 0, me.z)
        back(j, 1, me.z)

    def gather_step(j, t):
        for direction, half, steps in STREAMS:
            if t < steps:
                gathers[j, direction, half, t].wait_recv()
                if t + 1 < steps:
                    gather(j, direction, half, t + 1)
                back(j, half, level(-direction * (t + 1)))
        if t == 3:
            from_sibling[j] = push(
                full[j].at[:, :, 1 - me.c], sib_in[j], sib_send.at[j], sib_recv.at[j], me.sibling()
            )

    def weight_rows(j, half, g, raw):
        cut = slice(G * g, G * g + G)
        ours = full[j][:, half, me.c, cut, :].reshape(256, CHUNKS[j])
        theirs = sib_in[j][:, half, cut, :].reshape(256, CHUNKS[j])
        total = dot(back_table[me.c, 0], ours) + dot(back_table[me.c, 1], ours)
        total = total + (dot(back_table[1 - me.c, 0], theirs) + dot(back_table[1 - me.c, 1], theirs))
        probs[me.c] += dot(raw, ours, NT)
        probs[1 - me.c] += dot(raw, theirs, NT)
        return total.reshape(16, G, CHUNKS[j]).astype(BF16)

    def weights(j):
        from_sibling[j].wait_recv()
        for g in range(4):
            cut = slice(G * g, G * g + G)
            raw = far_in[j][:, cut, :].reshape(256, CHUNKS[j])
            gw_out[j][:, cut, :] = weight_rows(j, 1 - me.h, g, raw)
        to_far.append(push(gw_out[j], gw[j].at[me.h], out_send.at[j], out_recv.at[j], me.far()))
        for g in range(4):
            cut = slice(G * g, G * g + G)
            raw = w[j][:, cut, :].reshape(256, CHUNKS[j])
            gw[j][me.h, :, cut, :] = weight_rows(j, me.h, g, raw)

    stages = [functools.partial(reduce_step, t=t) for t in range(4)]
    stages += [activate] + [functools.partial(gather_step, t=t) for t in range(4)] + [weights]
    for tick in range(len(stages) + 2 * LEAD):
        for j in range(3):
            stage = tick - LEAD * j
            if stage == 0:
                ready(j)
            if 0 <= stage < len(stages):
                stages[stage](j)

    experts = one_hot((256, 128), G, 1, F32)
    local = jnp.zeros((32, 128), F32)
    for seg_core in range(2):
        kept = jnp.where(mask, probs[seg_core], 0.0)
        segments = jnp.where(pick(seg_core), 1.0, 0.0)
        local = local + dot(segments, dot(kept, experts, TN, HIGHEST), TN, HIGHEST)

    def sum_start(value, used, base, place, count, peer):
        ring[base + place] = value
        block = ring.at[base + place]
        return [
            push(block, block, p_send.at[used + i - 1], p_recv.at[used + i - 1], peer(i)) for i in range(1, count)
        ]

    def sum_end(copies, base, count):
        for copy in copies:
            copy.wait_recv()
        total = ring[base]
        for i in range(1, count):
            total = total + ring[base + i]
        return total

    def slice_of(y):
        row = pl.multiple_of(128 * ((y % 4) // 2), 128)
        return half_sum.at[2 * (y // 4) + y % 2, pl.ds(row, 128), :]

    def sum_x(lead):
        total = rows[lead, me.x].astype(F32)
        for step in range(1, NX):
            i = 4 * (step - 1) + lead
            block = rows_in.at[step - 1, lead]
            remote(block, block, rx_send.at[i], rx_recv.at[i], me.at_x(step)).wait_recv()
            total = total + rows_in[step - 1, lead].astype(F32)
        half_sum[lead] = total.astype(BF16)
        first = 4 * (lead // 2) + lead % 2
        for y in (first, first + 2):

            @pl.when(y != me.y)
            def _():
                remote(
                    slice_of(y), slices_in.at[me.y], ry_send.at[y], ry_recv.at[me.y], me.at(h=y // 4, e=y % 4)
                ).start()

    copies = sum_start(local, 0, 0, me.c, 2, lambda i: me.sibling())
    sum_x(0)
    value = sum_end(copies, 0, 2)
    copies = sum_start(value, 1, 2, me.x, NX, me.at_x)
    sum_x(1)
    value = sum_end(copies, 2, NX)
    copies = sum_start(value, 4, 6, me.y, NY, me.at_y)
    sum_x(2)
    sum_x(3)
    value = sum_end(copies, 6, NY)
    copies = sum_start(value, 11, 14, me.z, NZ, me.at_z)
    total = slice_of(me.y)[...].astype(F32)
    for i in range(1, NY):
        y = (me.y + i) % NY
        block = slices_in.at[y]
        remote(block, block, ry_send.at[y], ry_recv.at[y], me.at_y(i)).wait_recv()
        total = total + slices_in[y].astype(F32)
    done[...] = total.astype(BF16)
    swap_start(swap, done, home, swap2)
    to_far[0].wait_recv()
    to_far[1].wait_recv()
    for lo in range(0, 16, 4):
        at = slice(lo, lo + 4)
        for half in range(2):
            tile = slice(128 * half, 128 * half + 128)
            first, second = gw[0][half, at], gw[1][half, at]
            gg_ref[at, :, tile] = jnp.concatenate([first[..., :64], second[..., :64]], axis=-1)
            gu_ref[at, :, tile] = jnp.concatenate([first[..., 64:], second[..., 64:]], axis=-1)
    gp_ref[...] = sum_end(copies, 14, NZ).T[:16]
    to_far[2].wait_recv()
    for lo in range(0, 16, 4):
        at = slice(lo, lo + 4)
        first, second = gw[2][0, at], gw[2][1, at]
        gg_ref[at, :, 256:352] = jnp.concatenate([first[..., :48], second[..., :48]], axis=-1)
        gu_ref[at, :, 256:352] = jnp.concatenate([first[..., 48:], second[..., 48:]], axis=-1)
    swap_wait(swap, done, home, swap2)
    gt_ref[...] = home[...].T
    for copy in sent:
        copy.wait_send()
    for i in range(1, NY):
        y = (me.y + i) % NY
        remote(slice_of(y), slices_in.at[me.y], ry_send.at[y], ry_recv.at[me.y], me.at_y(i)).wait_send()
    for step in range(1, NX):
        for lead in range(4):
            i = 4 * (step - 1) + lead
            block = rows_in.at[step - 1, lead]
            remote(block, block, rx_send.at[i], rx_recv.at[i], me.at_x(step)).wait_send()


def shape(*dims, dtype=BF16):
    return jax.ShapeDtypeStruct(dims, dtype)


def buffers(*dims):
    return pltpu.VMEM(dims, BF16)


def per_chunk(*dims):
    return [buffers(*[width if d is None else d for d in dims]) for width in CHUNKS]


def shards(tokens, grad_hidden, merge_probs, w_gate, w_up):
    out_shape = [shape(256, 128), shape(16, 64, 352), shape(16, 64, 352), shape(16, 32, dtype=F32)]
    scratch = [
        buffers(16, 64, 352), buffers(16, 64, 352), buffers(256, 128),
        pltpu.VMEM((16, 32), F32), DMA((5,)), buffers(128, 256), buffers(352, 256),
        *per_chunk(16, 64, None), *per_chunk(16, 64, None), *per_chunk(2, 16, 64, None),
        buffers(2, 2, 256, 256), buffers(2, 2, 256, 256), buffers(4, 4, 256, 256), buffers(176, 256),
        pltpu.VMEM((2, 256, 256), F32), pltpu.VMEM((22, 32, 128), F32),
        *per_chunk(16, 64, None), *per_chunk(2, 16, 64, None), *per_chunk(16, 256, None),
        *per_chunk(14, None, 256), *per_chunk(14, None, 256), *per_chunk(2, 8, None, 256),
        *per_chunk(16, 2, 2, 64, None), *per_chunk(16, 2, 64, None), *per_chunk(16, 64, None),
        buffers(4, 4, 256, 256), buffers(3, 4, 256, 256), buffers(4, 256, 256), buffers(8, 128, 256),
        buffers(128, 256), buffers(128, 256),
    ]
    counts = [3, 3, 7, 7, 24, 24, 3, 3, 6, 6, 4, 42, 42, 42, 42, 3, 3, 3, 3, 12, 12, 8, 8, 18, 18]
    operands = [w_gate, w_up, tokens, grad_hidden.T, merge_probs.T]
    grad_tokens, grad_gate, grad_up, grad_probs = pl.pallas_call(
        whole_kernel,
        out_shape=out_shape,
        in_specs=[pl.BlockSpec(memory_space=pl.ANY)] * len(operands),
        out_specs=[VMEM] * len(out_shape),
        scratch_shapes=scratch + [DMA((n,)) for n in counts],
        compiler_params=pltpu.CompilerParams(
            collective_id=1, has_side_effects=True, vmem_limit_bytes=56 * 1024 * 1024
        ),
        cost_estimate=pl.CostEstimate(flops=6 << 30, bytes_accessed=16 << 20, transcendentals=0),
    )(*operands)
    return grad_tokens, grad_gate, grad_up, grad_probs.T


def solution(mesh):
    return jax.shard_map(
        shards,
        mesh=mesh,
        in_specs=(
            P("dp", ("expert", "tensor")),
            P("dp", ("expert", "tensor")),
            P(),
            P(None, "dp", ("expert", "tensor")),
            P(None, "dp", ("expert", "tensor")),
        ),
        out_specs=(
            P("dp", ("expert", "tensor")),
            P(None, "dp", ("expert", "tensor")),
            P(None, "dp", ("expert", "tensor")),
            P(),
        ),
        check_vma=False,
    )
```
